128 devices in a mesh: var: 8 (over x, y_lo), space: 16 (over z, y_hi, core).
Axes of the slice: x: 4, y: 4 (y_hi: 2, y_lo: 2; y = y_hi * 2 + y_lo), z: 4, core: 2. Of those that a mesh axis runs over, the one named last changes fastest.
Arguments:
- pixels: bfloat16 [64, 1024, 4096], P('var', 'space'), may hold values from -6 to 6
- counts: int32 [64, 64, 256], P('var', 'space'), may hold values from 0 to 256
- embed_weight: bfloat16 [64, 32, 32, 512], P('var'), may hold values from -0.1875 to 0.1875
- var_embed: bfloat16 [64, 512], P('var'), may hold values from -3 to 3
- query: float32 [512], replicated, may hold values from -140 to 140
- key_weight: bfloat16 [512, 512], replicated, may hold values from -0.25 to 0.25
- value_weight: bfloat16 [512, 512], replicated, may hold values from -0.25 to 0.25
- out_weight: bfloat16 [512, 512], replicated, may hold values from -0.25 to 0.25
Outputs:
- aggregated: bfloat16 [64, 256, 512], P('space', 'var')
The draws below stay inside these ranges and needn't reach their ends.
All inputs are finite; a program needn't handle non-finite values.
Results may differ from the reference program's by a relative error of at most 0.011.
Values may be sent and summed in bfloat16 or wider, within the bound.
No kernel may reach another device: no remote copies, remote signals or barrier semaphores. Data moves between devices by JAX's collectives and lax.ppermute only.
A program may use at most 128 MiB of HBM per device.

```python
import math
import jax
import jax.numpy as jnp
from jax import lax

D = 512
HEADS = 8
PATCH = 16
KS = 32
VARS = 64
COLS = 4096
ROWS = 1024
PR = 64
PC = 256


def draw_query(key, part):
    key = jax.random.fold_in(key, 5)
    first_key = jax.random.fold_in(key, 0)
    base = jax.random.normal(first_key, (D,), jnp.float32)
    return base


def touch_ends(values, stream_key, low, top_value):
    longest = values.shape.index(max(values.shape))
    spots = []
    for shift in (0, 1):
        where = [jax.random.randint(jax.random.fold_in(stream_key, axis), (), 0, length) for axis, length in enumerate(values.shape)]
        where[longest] = (where[longest] + shift) % values.shape[longest]
        spots.append(tuple(where))
    return values.at[spots[0]].set(low).at[spots[1]].set(top_value)


def level_of(own_key, extent, pieces, smallest, top_value):
    gain = 1.0
    for axis_at, shards_of in pieces:
        heights = jax.random.uniform(jax.random.fold_in(jax.random.fold_in(own_key, 6), axis_at), (shards_of,), jnp.float32, smallest / len(pieces), top_value / len(pieces))
        gain = gain * jnp.repeat(jnp.exp(heights), extent[axis_at] // shards_of).reshape((-1,) + (1,) * (len(extent) - 1 - axis_at))
    return gain


def normal_values(stream_key, dims, scale, reach, pieces=(), kind=jnp.bfloat16):
    array = jax.random.normal(stream_key, dims, jnp.float32) * scale
    if len(pieces) > 0:
        array = level_of(stream_key, dims, pieces, -0.22, 0.18) * array
    return jnp.clip(array, min=-reach, max=reach).astype(kind)


def setup_inputs(seed: int = 0) -> dict:
    splits = jax.random.split(jax.random.key(seed), 9)
    return {
        "pixels": normal_values(splits[0], (VARS, ROWS, COLS), 1.0, 6.0, ((0, 8), (1, 16))),
        "counts": touch_ends(jax.random.randint(splits[1], (VARS, PR, PC), 0, PATCH * PATCH + 1), jax.random.fold_in(splits[1], 1), 0, PATCH * PATCH).astype(jnp.int32),
        "embed_weight": normal_values(splits[2], (VARS, KS, KS, D), (KS * KS) ** -0.5, 0.1875, ((0, 8),)),
        "var_embed": normal_values(splits[3], (VARS, D), 0.5, 3.0, ((0, 8),)),
        "query": draw_query(jax.random.fold_in(splits[8], 71), 0),
        "key_weight": normal_values(splits[5], (D, D), D ** -0.5, 0.25),
        "value_weight": normal_values(splits[6], (D, D), D ** -0.5, 0.25),
        "out_weight": normal_values(splits[7], (D, D), D ** -0.5, 0.25),
    }


def cell_blocks(raster):
    row_count, col_count = raster.shape
    row_cells = row_count // PATCH
    col_cells = col_count // PATCH
    shaped = raster.reshape(row_cells, PATCH, col_cells, PATCH).transpose(0, 2, 1, 3)
    return shaped.reshape(row_cells, col_cells, PATCH * PATCH)

def embed_one(raster, kernel, offset):
    blocks = cell_blocks(raster)
    model_width = kernel.shape[-1]
    kernel_parts = kernel.reshape(2, PATCH, 2, PATCH, model_width).transpose(0, 2, 1, 3, 4)
    kernel_parts = kernel_parts.reshape(2, 2, PATCH * PATCH, model_width)
    patch_rows = blocks.shape[0] - 1
    patch_cols = blocks.shape[1] - 1
    summed = jnp.zeros((patch_rows, patch_cols, model_width), jnp.float32) + offset.astype(jnp.float32)
    for a in range(2):
        for b in range(2):
            segment = blocks[a:a + patch_rows, b:b + patch_cols].reshape(patch_rows * patch_cols, PATCH * PATCH)
            product = jnp.dot(segment, kernel_parts[a, b], preferred_element_type=jnp.float32)
            summed = summed + product.reshape(patch_rows, patch_cols, model_width)
    return summed.astype(jnp.bfloat16)

def reference(pixels, counts, embed_weight, var_embed, query, key_weight, value_weight, out_weight):
    head_size = D // HEADS
    half = PATCH // 2
    key_query = lax.optimization_barrier(jnp.sum(key_weight.astype(jnp.float32).reshape(D, HEADS, head_size) * query.reshape(HEADS, head_size), -1)) / math.sqrt(head_size)
    patch_rows = pixels.shape[1] // PATCH
    patch_cols = pixels.shape[2] // PATCH

    def absorb(carry, members):
        highest, totals, weighted = carry
        raster, valid, kernel, offset = members
        framed = jnp.pad(raster, ((half, half), (half, half)))
        tokens = embed_one(framed, kernel, offset).astype(jnp.float32).reshape(patch_rows * patch_cols, D)
        scores = jnp.dot(tokens, key_query, precision=lax.Precision.HIGHEST).reshape(patch_rows, patch_cols, HEADS)
        scores = scores + jnp.log((1.0 + valid.astype(jnp.float32)) / (1.0 + PATCH * PATCH))[..., None]
        newest = jnp.maximum(highest, scores)
        decay_old = jnp.exp(highest - newest)
        fresh = jnp.exp(scores - newest)
        totals = totals * decay_old + fresh
        weighted = weighted * decay_old[..., None] + fresh[..., None] * tokens.reshape(patch_rows, patch_cols, 1, D)
        return ((newest, totals, weighted), None)
    start = (jnp.full((patch_rows, patch_cols, HEADS), -1e+30, jnp.float32), jnp.zeros((patch_rows, patch_cols, HEADS), jnp.float32), jnp.zeros((patch_rows, patch_cols, HEADS, D), jnp.float32))
    (highest, totals, weighted), _ = lax.scan(absorb, start, (pixels, counts, embed_weight, var_embed))
    value_heads = value_weight.astype(jnp.float32).reshape(D, HEADS, head_size)
    mixed = jnp.einsum('phd,dhe->phe', weighted.reshape(-1, HEADS, D), value_heads, precision=lax.Precision.HIGHEST)
    mixed = mixed / totals.reshape(-1, HEADS, 1)
    mixture = mixed.reshape(-1, D).astype(jnp.bfloat16)
    result = jnp.dot(mixture, out_weight, preferred_element_type=jnp.float32)
    return result.reshape(patch_rows, patch_cols, D).astype(jnp.bfloat16)
```

```python
import functools
import math

import jax
import jax.numpy as jnp
from jax import lax
from jax.experimental import pallas as pl
from jax.experimental.pallas import tpu as pltpu
from jax.sharding import PartitionSpec as P

HEADS = 8
HEAD = 64
PATCH = 16
D = 512
COLS = 4096
PC = 256
LANES = 128
TILES = COLS // LANES
VPD = 8
DEVS = 8
OWN = PC // DEVS
BF = jnp.bfloat16
F32 = jnp.float32
NT = (((1,), (1,)), ((), ()))


def three_parts(x):
    high = x.astype(BF)
    rest = x - high.astype(F32)
    middle = rest.astype(BF)
    return high, middle, (rest - middle.astype(F32)).astype(BF)


def relayout_group(rows, stage, put):
    for t in range(TILES):
        stage[t * 8 : t * 8 + 8, :] = rows[:, t * LANES : (t + 1) * LANES]
    skewed = []
    for r in range(8):
        g = stage[pl.ds(r, TILES, stride=8), :].astype(BF)
        skewed.append(pltpu.roll(g, 16 * r, 1) if r else g)
    lane = lax.broadcasted_iota(jnp.int32, (TILES, LANES), 1)
    level = [skewed[(-k) % 8] for k in range(8)]
    for bit in (1, 2, 4):
        chosen = ((lane // 16) & bit) != 0
        level = [jnp.where(chosen, level[(k - bit) % 8], level[k]) for k in range(8)]
    low = [pltpu.roll(level[k], (-16 * k - 8) % LANES, 1) for k in range(8)]
    high = [pltpu.roll(level[k], (-16 * k + 8) % LANES, 1) for k in range(8)]
    sub = lax.broadcasted_iota(jnp.int32, (TILES, LANES), 0)
    before = jnp.where(sub == 0, 0.0, pltpu.roll(low[7].astype(F32), 1, 0)).astype(BF)
    after = jnp.where(sub == TILES - 1, 0.0, pltpu.roll(high[0].astype(F32), TILES - 1, 0)).astype(BF)
    first = (lane % 16) < 8
    for k in range(8):
        put(k, 0, jnp.where(first, low[k - 1] if k else before, high[k]))
        put(k, 1, jnp.where(first, low[k], high[k + 1] if k < 7 else after))


def permutation():
    row = lax.broadcasted_iota(jnp.int32, (PC, PC), 0)
    col = lax.broadcasted_iota(jnp.int32, (PC, PC), 1)
    same = ((row // 8) == (col % TILES)) & ((row % 8) == (col // TILES))
    return jnp.where(same, 1.0, 0.0).astype(BF)


def embed_kernel(edge, *refs):
    if edge:
        low_ref, high_ref, *refs = refs
    (px_ref, cnt_ref, w_ref, ve_ref, q_ref, kw_ref, vwt_ref, msg_ref,
     a_ref, stage, ext, top_ref, tot_ref, acc_ref) = refs
    step = pl.program_id(0)

    @pl.when(step == 0)
    def _():
        head = lax.broadcasted_iota(jnp.int32, (HEADS, D), 0)
        col = lax.broadcasted_iota(jnp.int32, (HEADS, D), 1)
        spread = jnp.where(col // HEAD == head, jnp.broadcast_to(q_ref[...], (HEADS, D)), 0.0)
        parts = lax.dot_general(jnp.concatenate(three_parts(spread), 0), kw_ref[...], NT, preferred_element_type=F32)
        kq = (parts[0:8] + parts[8:16] + parts[16:24]) / math.sqrt(HEAD)
        ext[0:D, :] = vwt_ref[...]
        ext[D : D + 32, :] = jnp.concatenate((*three_parts(kq), jnp.zeros((8, D), BF)), 0)
        top_ref[...] = jnp.full_like(top_ref, -1e30)
        tot_ref[...] = jnp.zeros_like(tot_ref)
        acc_ref[...] = jnp.zeros_like(acc_ref)

    if edge:
        body = px_ref[0].astype(F32)
        groups = [low_ref[0].astype(F32), body[0:8], body[8:16], body[16:24],
                  body[40:48], body[48:56], body[56:64], high_ref[0].astype(F32)]
        starts, rows = (0, 4), (0, 3)
    else:
        body = px_ref[0].astype(F32)
        groups = [body[8 * n : 8 * n + 8] for n in range(1, 7)]
        starts, rows = (0, 2), (1, 2)
    for n, group in enumerate(groups):
        def put(k, half, x, n=n):
            a_ref[n, k * TILES : (k + 1) * TILES, half * LANES : (half + 1) * LANES] = x
        relayout_group(group, stage.at[n], put)
    w = jnp.concatenate(
        [w_ref[0, 8 * g : 8 * g + 8, 16 * b : 16 * b + 16, :].reshape(LANES, D) for g in range(4) for b in range(2)], 0
    )
    which = lax.broadcasted_iota(jnp.int32, (VPD, D), 0) == step
    offset = jnp.sum(jnp.where(which, ve_ref[...].astype(F32), 0.0), 0, keepdims=True)
    perm = permutation()
    for n, (start, row) in enumerate(zip(starts, rows)):
        a = jnp.concatenate([a_ref[start + g] for g in range(4)], 1)
        tokens = (jnp.dot(a, w, preferred_element_type=F32) + offset).astype(BF)
        both = lax.dot_general(ext[...], tokens, NT, preferred_element_type=F32)
        valid = jnp.dot(
            jnp.broadcast_to(cnt_ref[0, row : row + 1, :].astype(F32), (8, PC)).astype(BF), perm,
            preferred_element_type=F32,
        )
        scores = both[D : D + 8] + both[D + 8 : D + 16] + both[D + 16 : D + 24]
        scores = scores + jnp.log((1.0 + valid) / (1.0 + PATCH * PATCH))
        old = top_ref[n]
        top = jnp.maximum(old, scores)
        decay = jnp.exp(old - top)
        fresh = jnp.exp(scores - top)
        top_ref[n] = top
        tot_ref[n] = tot_ref[n] * decay + fresh
        for h in range(HEADS):
            at = slice(h * HEAD, (h + 1) * HEAD)
            acc_ref[n, at, :] = acc_ref[n, at, :] * decay[h : h + 1] + both[at] * fresh[h : h + 1]

    @pl.when(step == VPD - 1)
    def _():
        lane = lax.broadcasted_iota(jnp.int32, (24, LANES), 1)
        sums = []
        for n in range(2):
            total = tot_ref[n]
            weighted = jnp.concatenate(
                [acc_ref[n, h * HEAD : (h + 1) * HEAD, :] / total[h : h + 1] for h in range(HEADS)], 0
            ).astype(BF)
            natural = lax.dot_general(perm, weighted, NT, preferred_element_type=F32).astype(BF)
            for d in range(DEVS):
                msg_ref[d, n * OWN : (n + 1) * OWN, :] = natural[d * OWN : (d + 1) * OWN]
            parts = jnp.concatenate(three_parts(top_ref[n] + jnp.log(total)), 0)
            sums.append(lax.dot_general(parts, perm, NT, preferred_element_type=F32))
        for d in range(DEVS):
            spot = d * OWN // LANES * LANES
            picked = jnp.zeros((24, LANES), F32)
            for n in range(2):
                moved = pltpu.roll(sums[n][:, spot : spot + LANES], (n * OWN - d * OWN) % LANES, 1)
                picked = jnp.where(lane // OWN == n, moved, picked)
            wide = jnp.concatenate([picked[0:8], picked[8:16], picked[16:24], jnp.zeros((8, LANES), F32)], 1)
            msg_ref[d, 2 * OWN : 2 * OWN + 16, :] = jnp.concatenate([wide, jnp.zeros((8, D), F32)], 0).astype(BF)


def embed(pixels, halos, counts, weight, var_embed, query, key_weight, value_turned):
    edge = halos is not None
    groups = 8 if edge else 6
    whole = lambda *shape: pl.BlockSpec(shape, lambda v: (0,) * len(shape))
    halo_spec = [pl.BlockSpec((1, 8, COLS), lambda v: (v, 0, 0))] * 2 if edge else []
    return pl.pallas_call(
        functools.partial(embed_kernel, edge),
        grid=(VPD,),
        in_specs=halo_spec + [
            pl.BlockSpec((1, 64, COLS), lambda v: (v, 0, 0)),
            pl.BlockSpec((1, 4, PC), lambda v: (v, 0, 0)),
            pl.BlockSpec((1, 32, 32, D), lambda v: (v, 0, 0, 0)),
            whole(VPD, D), whole(1, D), whole(D, D), whole(D, D),
        ],
        out_specs=whole(DEVS, 2 * OWN + 16, D),
        out_shape=jax.ShapeDtypeStruct((DEVS, 2 * OWN + 16, D), BF),
        scratch_shapes=[
            pltpu.VMEM((groups, PC, PC), BF),
            pltpu.VMEM((groups, TILES * 8, LANES), F32),
            pltpu.VMEM((D + 32, D), BF),
            pltpu.VMEM((2, HEADS, PC), F32),
            pltpu.VMEM((2, HEADS, PC), F32),
            pltpu.VMEM((2, D, PC), F32),
        ],
        compiler_params=pltpu.CompilerParams(vmem_limit_bytes=40 * 2**20),
        cost_estimate=pl.CostEstimate(flops=8 * 2 * 512 * (1024 + 512) * 512, bytes_accessed=13 * 2**20, transcendentals=0),
        name="embed_edge" if edge else "embed_inner",
    )(*(halos or ()), pixels, counts, weight, var_embed, query, key_weight, value_turned)


def finish_kernel(inner_ref, outer_ref, wo_ref, out_ref):
    head = lax.broadcasted_iota(jnp.int32, (HEADS, D), 0)
    col = lax.broadcasted_iota(jnp.int32, (HEADS, D), 1)
    one = jnp.where(col // HEAD == head, 1.0, 0.0).astype(BF)
    spread = jnp.concatenate((one, one), 0)
    for ref, rows in ((inner_ref, (1, 2)), (outer_ref, (0, 3))):
        sums = []
        for s in range(DEVS):
            wide = ref[s, 2 * OWN : 2 * OWN + 16, :].astype(F32)[0:8]
            sums.append(wide[:, 0:LANES] + wide[:, LANES : 2 * LANES] + wide[:, 2 * LANES : 3 * LANES])
        top = functools.reduce(jnp.maximum, sums)
        parts = [jnp.exp(x - top) for x in sums]
        scale = 1.0 / functools.reduce(jnp.add, parts)
        mixture = jnp.zeros((2 * OWN, D), F32)
        for s in range(DEVS):
            share = parts[s] * scale
            high = share.astype(BF)
            low = (share - high.astype(F32)).astype(BF)
            wide = lax.dot_general(jnp.concatenate((high, low), 0), spread, (((0,), (0,)), ((), ())), preferred_element_type=F32)
            mixture = mixture + wide[0 : 2 * OWN] * ref[s, 0 : 2 * OWN, :].astype(F32)
        result = jnp.dot(mixture.astype(BF), wo_ref[...], preferred_element_type=F32).astype(BF)
        for n, row in enumerate(rows):
            out_ref[row] = result[n * OWN : (n + 1) * OWN]


def finish(inner, outer, out_weight):
    return pl.pallas_call(
        finish_kernel,
        out_shape=jax.ShapeDtypeStruct((4, OWN, D), BF),
        compiler_params=pltpu.CompilerParams(vmem_limit_bytes=24 * 2**20),
        name="finish",
    )(inner, outer, out_weight)


def exchange(msg):
    return lax.all_to_all(msg, "var", 0, 0)


def shards(pixels, counts, embed_weight, var_embed, query, key_weight, value_weight, out_weight):
    count = lax.axis_size("space")
    forward = [(i, i + 1) for i in range(count - 1)]
    low = lax.ppermute(pixels[:, 56:64], "space", forward)
    high = lax.ppermute(pixels[:, 0:8], "space", [(b, a) for a, b in forward])
    rest = (counts, embed_weight, var_embed, query.reshape(1, D), key_weight, value_weight.T)
    inner = exchange(embed(pixels, None, *rest))
    outer = exchange(embed(pixels, (low, high), *rest))
    return finish(inner, outer, out_weight)


def solution(mesh):
    return jax.shard_map(
        shards,
        mesh=mesh,
        in_specs=(
            P("var", "space", None),
            P("var", "space", None),
            P("var", None, None, None),
            P("var", None),
            P(),
            P(),
            P(),
            P(),
        ),
        out_specs=P("space", "var", None),
        check_vma=False,
    )
```

```python
import functools
import math

import jax
import jax.numpy as jnp
from jax import lax
from jax.experimental import pallas as pl
from jax.experimental.pallas import tpu as pltpu
from jax.sharding import PartitionSpec as P

HEADS = 8
HEAD = 64
PATCH = 16
D = 512
COLS = 4096
PC = 256
LANES = 128
TILES = COLS // LANES
VPD = 8
DEVS = 8
OWN = PC // DEVS
BF = jnp.bfloat16
F32 = jnp.float32
NT = (((1,), (1,)), ((), ()))


def three_parts(x):
    high = x.astype(BF)
    rest = x - high.astype(F32)
    middle = rest.astype(BF)
    return high, middle, (rest - middle.astype(F32)).astype(BF)


def relayout_group(rows, stage, edge_stage, out):
    for t in range(TILES):
        stage[t * 8 : t * 8 + 8, :] = rows[:, t * LANES : (t + 1) * LANES]
    skewed = [
        pltpu.roll(stage[pl.ds(r, TILES, stride=8), :].astype(BF), (16 * r + 8) % LANES, 1) for r in range(8)
    ]
    lane = lax.broadcasted_iota(jnp.int32, (TILES, LANES), 1)
    level = [skewed[(-k) % 8] for k in range(8)]
    for bit in (1, 2, 4):
        chosen = ((lane // 16) & bit) != 0
        level = [jnp.where(chosen, level[(k - bit) % 8], level[k]) for k in range(8)]
    for k in range(1, 8):
        out[k * TILES : (k + 1) * TILES, :] = pltpu.roll(level[k], (-16 * k) % LANES, 1)
    edge_stage[8 : 8 + TILES, :] = level[0].astype(F32)
    left = (lane % 16) < 8
    out[0:TILES, :] = jnp.where(left, edge_stage[7 : 7 + TILES, :].astype(BF), level[0])
    out[8 * TILES : 9 * TILES, :] = jnp.where(left, level[0], edge_stage[9 : 9 + TILES, :].astype(BF))


def permutation():
    row = lax.broadcasted_iota(jnp.int32, (PC, PC), 0)
    col = lax.broadcasted_iota(jnp.int32, (PC, PC), 1)
    same = ((row // 8) == (col % TILES)) & ((row % 8) == (col // TILES))
    return jnp.where(same, 1.0, 0.0).astype(BF)


def embed_kernel(edge, *refs):
    if edge:
        low_hbm, high_hbm, ext_hbm, *refs = refs
    else:
        query_ref, key_hbm, value_hbm, *refs = refs
    px_hbm, w_hbm, cnt_ref, ve_ref, msg_ref, *refs = refs
    if not edge:
        ext_out, *refs = refs
    (px, w, ext, a_even, a_odd, stage_even, stage_odd, edges, bias_ref, off_ref, top_ref, tot_ref, acc_ref, px_sem, w_sem,
     *more) = refs
    if not edge:
        key_ref, value_ref = more[1:]
    rows = (0, 3) if edge else (1, 2)
    starts = (0, 4) if edge else (0, 2)

    def px_copies(v):
        copies = [pltpu.make_async_copy(px_hbm.at[v], px.at[v], px_sem.at[v])]
        if edge:
            low, high, halo_sem, _ = more
            copies.append(pltpu.make_async_copy(low_hbm.at[v], low.at[v], halo_sem.at[0, v]))
            copies.append(pltpu.make_async_copy(high_hbm.at[v], high.at[v], halo_sem.at[1, v]))
        return copies

    def w_copy(v):
        return pltpu.make_async_copy(w_hbm.at[v], w.at[v], w_sem.at[v])

    def fetch(v):
        for copy in px_copies(v):
            copy.start()
        w_copy(v).start()

    for copy in px_copies(0):
        copy.start()
    if edge:
        first_copies = [pltpu.make_async_copy(ext_hbm, ext, more[3].at[0])]
    else:
        first_copies = [
            pltpu.make_async_copy(key_hbm, key_ref, more[0].at[0]),
            pltpu.make_async_copy(value_hbm, value_ref, more[0].at[1]),
        ]
    for copy in first_copies:
        copy.start()
    w_copy(0).start()
    fetch(1)
    for copy in px_copies(2):
        copy.start()

    def relayout(v, a_ref, stage):
        body = px[v].astype(F32)
        if edge:
            groups = [more[0][v].astype(F32), body[0:8], body[8:16], body[16:24],
                      body[40:48], body[48:56], body[56:64], more[1][v].astype(F32)]
        else:
            groups = [body[8 * n : 8 * n + 8] for n in range(1, 7)]
        for n, group in enumerate(groups):
            relayout_group(group, stage.at[n], edges.at[n], a_ref.at[n])

    def compute(v, a_ref):
        a = jnp.concatenate(
            [
                jnp.concatenate([a_ref[start + g, b * TILES : b * TILES + PC, :] for g in range(4) for b in range(2)], 1)
                for start in starts
            ],
            0,
        )
        weight = jnp.concatenate(
            [w[v, 8 * g : 8 * g + 8, 16 * b : 16 * b + 16, :].reshape(LANES, D) for g in range(4) for b in range(2)], 0
        )
        tokens = (jnp.dot(a, weight, preferred_element_type=F32) + off_ref[v]).astype(BF)
        both = lax.dot_general(ext[...], tokens, NT, preferred_element_type=F32)
        scores = both[D : D + 8] + both[D + 8 : D + 16] + both[D + 16 : D + 24] + bias_ref[v]
        old = top_ref[...]
        top = jnp.maximum(old, scores)
        decay = jnp.exp(old - top)
        fresh = jnp.exp(scores - top)
        top_ref[...] = top
        tot_ref[...] = tot_ref[...] * decay + fresh
        for h in range(HEADS):
            at = slice(h * HEAD, (h + 1) * HEAD)
            acc_ref[at, :] = acc_ref[at, :] * decay[h : h + 1] + both[at] * fresh[h : h + 1]

    edges[...] = jnp.zeros_like(edges)
    perm = permutation()
    valid = jnp.concatenate([cnt_ref[v].astype(F32) for v in range(VPD)], 0).astype(BF)
    bias = jnp.log((1.0 + jnp.dot(valid, perm, preferred_element_type=F32)) / (1.0 + PATCH * PATCH))
    offsets = ve_ref[...].astype(F32)
    for v in range(VPD):
        off_ref[v] = offsets[v : v + 1]
        bias_ref[v] = jnp.concatenate([bias[4 * v + row : 4 * v + row + 1] for row in rows], 1)
    top_ref[...] = jnp.full_like(top_ref, -1e30)
    tot_ref[...] = jnp.zeros_like(tot_ref)
    acc_ref[...] = jnp.zeros_like(acc_ref)
    for copy in first_copies:
        copy.wait()
    if not edge:
        head = lax.broadcasted_iota(jnp.int32, (HEADS, D), 0)
        col = lax.broadcasted_iota(jnp.int32, (HEADS, D), 1)
        spread = jnp.where(col // HEAD == head, jnp.broadcast_to(query_ref[...], (HEADS, D)), 0.0)
        parts = lax.dot_general(jnp.concatenate(three_parts(spread), 0), key_ref[...], NT, preferred_element_type=F32)
        kq = (parts[0:8] + parts[8:16] + parts[16:24]) / math.sqrt(HEAD)
        ext[0:D, :] = value_ref[...].T
        ext[D : D + 32, :] = jnp.concatenate((*three_parts(kq), jnp.zeros((8, D), BF)), 0)
        ext_out[...] = ext[...]
    for copy in px_copies(0):
        copy.wait()
    relayout(0, a_even, stage_even)

    def pair(step, _):
        even = 2 * step
        later = jnp.minimum(even + 2, VPD - 1)

        @pl.when(step < VPD // 2 - 1)
        def _():
            w_copy(even + 2).start()
            fetch(even + 3)

        @pl.when(step < VPD // 2 - 2)
        def _():
            for copy in px_copies(even + 4):
                copy.start()

        w_copy(even).wait()
        w_copy(even + 1).wait()
        for copy in px_copies(even + 1):
            copy.wait()

        @pl.when(step < VPD // 2 - 1)
        def _():
            for copy in px_copies(even + 2):
                copy.wait()

        relayout(even + 1, a_odd, stage_odd)
        compute(even, a_even)
        relayout(later, a_even, stage_even)
        compute(even + 1, a_odd)
        return 0

    lax.fori_loop(0, VPD // 2, pair, 0)

    lane = lax.broadcasted_iota(jnp.int32, (24, LANES), 1)
    total = tot_ref[...]
    parts = jnp.concatenate(three_parts(top_ref[...] + jnp.log(total)), 0)
    sums = []
    for n in range(2):
        half = slice(n * PC, (n + 1) * PC)
        weighted = jnp.concatenate(
            [acc_ref[h * HEAD : (h + 1) * HEAD, half] / total[h : h + 1, half] for h in range(HEADS)], 0
        ).astype(BF)
        natural = lax.dot_general(perm, weighted, NT, preferred_element_type=F32).astype(BF)
        for d in range(DEVS):
            msg_ref[d, n * OWN : (n + 1) * OWN, :] = natural[d * OWN : (d + 1) * OWN]
        sums.append(lax.dot_general(parts[:, half], perm, NT, preferred_element_type=F32))
    for d in range(DEVS):
        spot = d * OWN // LANES * LANES
        picked = jnp.zeros((24, LANES), F32)
        for n in range(2):
            moved = pltpu.roll(sums[n][:, spot : spot + LANES], (n * OWN - d * OWN) % LANES, 1)
            picked = jnp.where(lane // OWN == n, moved, picked)
        wide = jnp.concatenate([picked[0:8], picked[8:16], picked[16:24], jnp.zeros((8, LANES), F32)], 1)
        msg_ref[d, 2 * OWN : 2 * OWN + 16, :] = jnp.concatenate([wide, jnp.zeros((8, D), F32)], 0).astype(BF)


def embed(edge, extras, pixels, weight, counts, var_embed):
    groups = 8 if edge else 6
    hbm = pl.BlockSpec(memory_space=pl.ANY)
    vmem = pl.BlockSpec(memory_space=pltpu.VMEM)
    out_shape = [jax.ShapeDtypeStruct((DEVS, 2 * OWN + 16, D), BF)]
    scratch = [
        pltpu.VMEM((VPD, 64, COLS), BF),
        pltpu.VMEM((VPD, 32, 32, D), BF),
        pltpu.VMEM((D + 32, D), BF),
        pltpu.VMEM((groups, PC + TILES, LANES), BF),
        pltpu.VMEM((groups, PC + TILES, LANES), BF),
        pltpu.VMEM((groups, TILES * 8, LANES), F32),
        pltpu.VMEM((groups, TILES * 8, LANES), F32),
        pltpu.VMEM((groups, TILES + 16, LANES), F32),
        pltpu.VMEM((VPD, 1, 2 * PC), F32),
        pltpu.VMEM((VPD, 1, D), F32),
        pltpu.VMEM((HEADS, 2 * PC), F32),
        pltpu.VMEM((HEADS, 2 * PC), F32),
        pltpu.VMEM((D, 2 * PC), F32),
        pltpu.SemaphoreType.DMA((VPD,)),
        pltpu.SemaphoreType.DMA((VPD,)),
    ]
    if edge:
        scratch += [
            pltpu.VMEM((VPD, 8, COLS), BF),
            pltpu.VMEM((VPD, 8, COLS), BF),
            pltpu.SemaphoreType.DMA((2, VPD)),
            pltpu.SemaphoreType.DMA((1,)),
        ]
    else:
        scratch += [pltpu.SemaphoreType.DMA((2,)), pltpu.VMEM((D, D), BF), pltpu.VMEM((D, D), BF)]
        out_shape.append(jax.ShapeDtypeStruct((D + 32, D), BF))
    return pl.pallas_call(
        functools.partial(embed_kernel, edge),
        in_specs=[hbm if edge else vmem, hbm, hbm, hbm, hbm, vmem, vmem],
        out_specs=[vmem] * len(out_shape),
        out_shape=out_shape,
        scratch_shapes=scratch,
        compiler_params=pltpu.CompilerParams(vmem_limit_bytes=56 * 2**20),
        cost_estimate=pl.CostEstimate(flops=8 * 2 * 512 * (1024 + 512) * 512, bytes_accessed=13 * 2**20, transcendentals=0),
        name="embed_edge" if edge else "embed_inner",
    )(*extras, pixels, weight, counts, var_embed)


def finish_kernel(inner_ref, outer_ref, wo_ref, out_ref):
    head = lax.broadcasted_iota(jnp.int32, (HEADS, D), 0)
    col = lax.broadcasted_iota(jnp.int32, (HEADS, D), 1)
    one = jnp.where(col // HEAD == head, 1.0, 0.0).astype(BF)
    spread = jnp.concatenate((one, one), 0)
    for ref, rows in ((inner_ref, (1, 2)), (outer_ref, (0, 3))):
        sums = []
        for s in range(DEVS):
            wide = ref[s, 2 * OWN : 2 * OWN + 16, :].astype(F32)[0:8]
            sums.append(wide[:, 0:LANES] + wide[:, LANES : 2 * LANES] + wide[:, 2 * LANES : 3 * LANES])
        top = functools.reduce(jnp.maximum, sums)
        parts = [jnp.exp(x - top) for x in sums]
        scale = 1.0 / functools.reduce(jnp.add, parts)
        mixture = jnp.zeros((2 * OWN, D), F32)
        for s in range(DEVS):
            share = parts[s] * scale
            high = share.astype(BF)
            low = (share - high.astype(F32)).astype(BF)
            wide = lax.dot_general(jnp.concatenate((high, low), 0), spread, (((0,), (0,)), ((), ())), preferred_element_type=F32)
            mixture = mixture + wide[0 : 2 * OWN] * ref[s, 0 : 2 * OWN, :].astype(F32)
        result = jnp.dot(mixture.astype(BF), wo_ref[...], preferred_element_type=F32).astype(BF)
        for n, row in enumerate(rows):
            out_ref[row] = result[n * OWN : (n + 1) * OWN]


def finish(inner, outer, out_weight):
    return pl.pallas_call(
        finish_kernel,
        out_shape=jax.ShapeDtypeStruct((4, OWN, D), BF),
        compiler_params=pltpu.CompilerParams(vmem_limit_bytes=24 * 2**20),
        name="finish",
    )(inner, outer, out_weight)


def exchange(msg):
    return lax.all_to_all(msg, "var", 0, 0)


def shards(pixels, counts, embed_weight, var_embed, query, key_weight, value_weight, out_weight):
    count = lax.axis_size("space")
    forward = [(i, i + 1) for i in range(count - 1)]
    low = lax.ppermute(pixels[:, 56:64], "space", forward)
    high = lax.ppermute(pixels[:, 0:8], "space", [(b, a) for a, b in forward])
    rest = (pixels, embed_weight, counts, var_embed)
    inner, ext = embed(False, (query.reshape(1, D), key_weight, value_weight), *rest)
    inner = exchange(inner)
    (outer,) = embed(True, (low, high, ext), *rest)
    outer = exchange(outer)
    return finish(inner, outer, out_weight)


def solution(mesh):
    return jax.shard_map(
        shards,
        mesh=mesh,
        in_specs=(
            P("var", "space", None),
            P("var", "space", None),
            P("var", None, None, None),
            P("var", None),
            P(),
            P(),
            P(),
            P(),
        ),
        out_specs=P("space", "var", None),
        check_vma=False,
    )
```

```python
import functools
import math

import jax
import jax.numpy as jnp
from jax import lax
from jax.experimental import pallas as pl
from jax.experimental.pallas import tpu as pltpu
from jax.sharding import PartitionSpec as P

HEADS = 8
HEAD = 64
PATCH = 16
D = 512
COLS = 4096
PC = 256
LANES = 128
TILES = COLS // LANES
VPD = 8
DEVS = 8
OWN = PC // DEVS
BF = jnp.bfloat16
F32 = jnp.float32
NT = (((1,), (1,)), ((), ()))


def three_parts(x):
    high = x.astype(BF)
    rest = x - high.astype(F32)
    middle = rest.astype(BF)
    return high, middle, (rest - middle.astype(F32)).astype(BF)


def relayout_group(rows, stage, edge_stage, out):
    for t in range(TILES):
        stage[t * 8 : t * 8 + 8, :] = rows[:, t * LANES : (t + 1) * LANES]
    skewed = [
        pltpu.roll(stage[pl.ds(r, TILES, stride=8), :].astype(BF), (16 * r + 8) % LANES, 1) for r in range(8)
    ]
    lane = lax.broadcasted_iota(jnp.int32, (TILES, LANES), 1)
    level = [skewed[(-k) % 8] for k in range(8)]
    for bit in (1, 2, 4):
        chosen = ((lane // 16) & bit) != 0
        level = [jnp.where(chosen, level[(k - bit) % 8], level[k]) for k in range(8)]
    for k in range(1, 8):
        out[k * TILES : (k + 1) * TILES, :] = pltpu.roll(level[k], (-16 * k) % LANES, 1)
    edge_stage[8 : 8 + TILES, :] = level[0].astype(F32)
    left = (lane % 16) < 8
    out[0:TILES, :] = jnp.where(left, edge_stage[7 : 7 + TILES, :].astype(BF), level[0])
    out[8 * TILES : 9 * TILES, :] = jnp.where(left, level[0], edge_stage[9 : 9 + TILES, :].astype(BF))


def permutation():
    row = lax.broadcasted_iota(jnp.int32, (PC, PC), 0)
    col = lax.broadcasted_iota(jnp.int32, (PC, PC), 1)
    same = ((row // 8) == (col % TILES)) & ((row % 8) == (col // TILES))
    return jnp.where(same, 1.0, 0.0).astype(BF)


def embed_kernel(edge, *refs):
    if edge:
        low_ref, high_ref, ext_hbm, *refs = refs
    else:
        query_hbm, key_hbm, value_hbm, *refs = refs
    px_hbm, w_hbm, cnt_hbm, ve_hbm, msg_ref, *refs = refs
    if not edge:
        ext_out, *refs = refs
    (px, w, ext, cnt_ref, ve_ref, a_even, a_odd, stage_even, stage_odd, edges, tok_even, tok_odd, bias_ref, off_ref,
     top_ref, tot_ref, acc_ref, px_sem, w_sem, sem, *more) = refs
    rows = (0, 3) if edge else (1, 2)
    starts = (0, 4) if edge else (0, 2)

    def px_copy(v):
        return pltpu.make_async_copy(px_hbm.at[v], px.at[v], px_sem.at[v])

    def w_copy(v):
        return pltpu.make_async_copy(w_hbm.at[v], w.at[v], w_sem.at[v])

    small = [(cnt_hbm, cnt_ref), (ve_hbm, ve_ref)]
    if edge:
        small.append((ext_hbm, ext))
    else:
        query_ref, key_ref, value_ref = more
        small += [(query_hbm, query_ref), (key_hbm, key_ref), (value_hbm, value_ref)]
    small = [pltpu.make_async_copy(src, dst, sem.at[n]) for n, (src, dst) in enumerate(small)]
    px_copy(0).start()
    for copy in small:
        copy.start()
    w_copy(0).start()
    px_copy(1).start()
    w_copy(1).start()
    px_copy(2).start()

    def relayout(v, a_ref, stage):
        body = px[v].astype(F32)
        if edge:
            groups = [low_ref[v].astype(F32), body[0:8], body[8:16], body[16:24],
                      body[40:48], body[48:56], body[56:64], high_ref[v].astype(F32)]
        else:
            groups = [body[8 * n : 8 * n + 8] for n in range(1, 7)]
        for n, group in enumerate(groups):
            relayout_group(group, stage.at[n], edges.at[n], a_ref.at[n])

    def embed_tokens(v, a_ref, tok):
        a = jnp.concatenate(
            [
                jnp.concatenate([a_ref[start + g, b * TILES : b * TILES + PC, :] for g in range(4) for b in range(2)], 1)
                for start in starts
            ],
            0,
        )
        weight = jnp.concatenate(
            [w[v, 8 * g : 8 * g + 8, 16 * b : 16 * b + 16, :].reshape(LANES, D) for g in range(4) for b in range(2)], 0
        )
        tok[...] = (jnp.dot(a, weight, preferred_element_type=F32) + off_ref[v]).astype(BF)

    def attend(v, tok):
        both = lax.dot_general(ext[...], tok[...], NT, preferred_element_type=F32)
        scores = both[0:8] + both[8:16] + both[16:24] + bias_ref[v + 1]
        old = top_ref[...]
        top = jnp.maximum(old, scores)
        decay = jnp.exp(old - top)
        fresh = jnp.exp(scores - top)
        top_ref[...] = top
        tot_ref[...] = tot_ref[...] * decay + fresh
        for h in range(HEADS):
            at = slice(h * HEAD, (h + 1) * HEAD)
            acc_ref[at, :] = acc_ref[at, :] * decay[h : h + 1] + both[32 + h * HEAD : 32 + (h + 1) * HEAD] * fresh[h : h + 1]

    edges[...] = jnp.zeros_like(edges)
    perm = permutation()
    small[0].wait()
    small[1].wait()
    valid = jnp.concatenate([cnt_ref[v].astype(F32) for v in range(VPD)], 0).astype(BF)
    bias = jnp.log((1.0 + jnp.dot(valid, perm, preferred_element_type=F32)) / (1.0 + PATCH * PATCH))
    offsets = ve_ref[...].astype(F32)
    for v in range(VPD):
        off_ref[v] = offsets[v : v + 1]
        bias_ref[v + 1] = jnp.concatenate([bias[4 * v + row : 4 * v + row + 1] for row in rows], 1)
    bias_ref[0] = jnp.full((1, 2 * PC), -1e30, F32)
    tok_odd[...] = jnp.zeros_like(tok_odd)
    top_ref[...] = jnp.full_like(top_ref, -1e30)
    tot_ref[...] = jnp.zeros_like(tot_ref)
    acc_ref[...] = jnp.zeros_like(acc_ref)
    for copy in small[2:]:
        copy.wait()
    if not edge:
        head = lax.broadcasted_iota(jnp.int32, (HEADS, D), 0)
        col = lax.broadcasted_iota(jnp.int32, (HEADS, D), 1)
        spread = jnp.where(col // HEAD == head, jnp.broadcast_to(query_ref[...], (HEADS, D)), 0.0)
        parts = lax.dot_general(jnp.concatenate(three_parts(spread), 0), key_ref[...], NT, preferred_element_type=F32)
        kq = (parts[0:8] + parts[8:16] + parts[16:24]) / math.sqrt(HEAD)
        ext[32 : D + 32, :] = value_ref[...].T
        ext[0:32, :] = jnp.concatenate((*three_parts(kq), jnp.zeros((8, D), BF)), 0)
        ext_copy = pltpu.make_async_copy(ext, ext_out, sem.at[0])
        ext_copy.start()
    px_copy(0).wait()
    relayout(0, a_even, stage_even)

    def pair(step, _):
        even = 2 * step
        later = jnp.minimum(even + 2, VPD - 1)

        @pl.when(step < VPD // 2 - 1)
        def _():
            w_copy(even + 2).start()
            px_copy(even + 3).start()
            w_copy(even + 3).start()

        @pl.when(step < VPD // 2 - 2)
        def _():
            px_copy(even + 4).start()

        w_copy(even).wait()
        w_copy(even + 1).wait()
        px_copy(even + 1).wait()

        @pl.when(step < VPD // 2 - 1)
        def _():
            px_copy(even + 2).wait()

        embed_tokens(even, a_even, tok_even)
        attend(even - 1, tok_odd)
        relayout(even + 1, a_odd, stage_odd)
        embed_tokens(even + 1, a_odd, tok_odd)
        attend(even, tok_even)
        relayout(later, a_even, stage_even)
        return 0

    lax.fori_loop(0, VPD // 2, pair, 0)
    attend(VPD - 1, tok_odd)
    if not edge:
        ext_copy.wait()

    lane = lax.broadcasted_iota(jnp.int32, (24, LANES), 1)
    total = tot_ref[...]
    parts = jnp.concatenate(three_parts(top_ref[...] + jnp.log(total)), 0)
    sums = []
    for n in range(2):
        half = slice(n * PC, (n + 1) * PC)
        weighted = jnp.concatenate(
            [acc_ref[h * HEAD : (h + 1) * HEAD, half] / total[h : h + 1, half] for h in range(HEADS)], 0
        ).astype(BF)
        natural = lax.dot_general(perm, weighted, NT, preferred_element_type=F32).astype(BF)
        for d in range(DEVS):
            msg_ref[d, n * OWN : (n + 1) * OWN, :] = natural[d * OWN : (d + 1) * OWN]
        sums.append(lax.dot_general(parts[:, half], perm, NT, preferred_element_type=F32))
    for d in range(DEVS):
        spot = d * OWN // LANES * LANES
        picked = jnp.zeros((24, LANES), F32)
        for n in range(2):
            moved = pltpu.roll(sums[n][:, spot : spot + LANES], (n * OWN - d * OWN) % LANES, 1)
            picked = jnp.where(lane // OWN == n, moved, picked)
        wide = jnp.concatenate([picked[0:8], picked[8:16], picked[16:24], jnp.zeros((8, LANES), F32)], 1)
        msg_ref[d, 2 * OWN : 2 * OWN + 16, :] = jnp.concatenate([wide, jnp.zeros((8, D), F32)], 0).astype(BF)


def embed(edge, extras, pixels, weight, counts, var_embed):
    groups = 8 if edge else 6
    hbm = pl.BlockSpec(memory_space=pltpu.HBM)
    vmem = pl.BlockSpec(memory_space=pltpu.VMEM)
    out_shape = [jax.ShapeDtypeStruct((DEVS, 2 * OWN + 16, D), BF)]
    scratch = [
        pltpu.VMEM((VPD, 64, COLS), BF),
        pltpu.VMEM((VPD, 32, 32, D), BF),
        pltpu.VMEM((D + 32, D), BF),
        pltpu.VMEM((VPD, 4, PC), jnp.int32),
        pltpu.VMEM((VPD, D), BF),
        pltpu.VMEM((groups, PC + TILES, LANES), BF),
        pltpu.VMEM((groups, PC + TILES, LANES), BF),
        pltpu.VMEM((groups, TILES * 8, LANES), F32),
        pltpu.VMEM((groups, TILES * 8, LANES), F32),
        pltpu.VMEM((groups, TILES + 16, LANES), F32),
        pltpu.VMEM((D, D), BF),
        pltpu.VMEM((D, D), BF),
        pltpu.VMEM((VPD + 1, 1, 2 * PC), F32),
        pltpu.VMEM((VPD, 1, D), F32),
        pltpu.VMEM((HEADS, 2 * PC), F32),
        pltpu.VMEM((HEADS, 2 * PC), F32),
        pltpu.VMEM((D, 2 * PC), F32),
        pltpu.SemaphoreType.DMA((VPD,)),
        pltpu.SemaphoreType.DMA((VPD,)),
        pltpu.SemaphoreType.DMA((5,)),
    ]
    if not edge:
        out_shape.append(jax.ShapeDtypeStruct((D + 32, D), BF))
        scratch += [pltpu.VMEM((1, D), F32), pltpu.VMEM((D, D), BF), pltpu.VMEM((D, D), BF)]
    return pl.pallas_call(
        functools.partial(embed_kernel, edge),
        in_specs=[vmem if edge else hbm] * 2 + [hbm] * 5,
        out_specs=[vmem, hbm][: len(out_shape)],
        out_shape=out_shape,
        scratch_shapes=scratch,
        compiler_params=pltpu.CompilerParams(vmem_limit_bytes=(48 if edge else 56) * 2**20),
        cost_estimate=pl.CostEstimate(flops=8 * 2 * 512 * (1024 + 512) * 512, bytes_accessed=13 * 2**20, transcendentals=0),
        name="embed_edge" if edge else "embed_inner",
    )(*extras, pixels, weight, counts, var_embed)


def finish_kernel(inner_ref, outer_ref, wo_ref, out_ref):
    head = lax.broadcasted_iota(jnp.int32, (HEADS, D), 0)
    col = lax.broadcasted_iota(jnp.int32, (HEADS, D), 1)
    one = jnp.where(col // HEAD == head, 1.0, 0.0).astype(BF)
    spread = jnp.concatenate((one, one), 0)
    for ref, rows in ((inner_ref, (1, 2)), (outer_ref, (0, 3))):
        sums = []
        for s in range(DEVS):
            wide = ref[s, 2 * OWN : 2 * OWN + 16, :].astype(F32)[0:8]
            sums.append(wide[:, 0:LANES] + wide[:, LANES : 2 * LANES] + wide[:, 2 * LANES : 3 * LANES])
        top = functools.reduce(jnp.maximum, sums)
        parts = [jnp.exp(x - top) for x in sums]
        scale = 1.0 / functools.reduce(jnp.add, parts)
        mixture = jnp.zeros((2 * OWN, D), F32)
        for s in range(DEVS):
            share = parts[s] * scale
            high = share.astype(BF)
            low = (share - high.astype(F32)).astype(BF)
            wide = lax.dot_general(jnp.concatenate((high, low), 0), spread, (((0,), (0,)), ((), ())), preferred_element_type=F32)
            mixture = mixture + wide[0 : 2 * OWN] * ref[s, 0 : 2 * OWN, :].astype(F32)
        result = jnp.dot(mixture.astype(BF), wo_ref[...], preferred_element_type=F32).astype(BF)
        for n, row in enumerate(rows):
            out_ref[row] = result[n * OWN : (n + 1) * OWN]


def finish(inner, outer, out_weight):
    return pl.pallas_call(
        finish_kernel,
        out_shape=jax.ShapeDtypeStruct((4, OWN, D), BF),
        compiler_params=pltpu.CompilerParams(vmem_limit_bytes=24 * 2**20),
        name="finish",
    )(inner, outer, out_weight)


def exchange(msg):
    return lax.all_to_all(msg, "var", 0, 0)


def shards(pixels, counts, embed_weight, var_embed, query, key_weight, value_weight, out_weight):
    count = lax.axis_size("space")
    forward = [(i, i + 1) for i in range(count - 1)]
    low = lax.ppermute(pixels[:, 56:64], "space", forward)
    high = lax.ppermute(pixels[:, 0:8], "space", [(b, a) for a, b in forward])
    rest = (pixels, embed_weight, counts, var_embed)
    inner, ext = embed(False, (query.reshape(1, D), key_weight, value_weight), *rest)
    inner = exchange(inner)
    (outer,) = embed(True, (low, high, ext), *rest)
    outer = exchange(outer)
    return finish(inner, outer, out_weight)


def solution(mesh):
    return jax.shard_map(
        shards,
        mesh=mesh,
        in_specs=(
            P("var", "space", None),
            P("var", "space", None),
            P("var", None, None, None),
            P("var", None),
            P(),
            P(),
            P(),
            P(),
        ),
        out_specs=P("space", "var", None),
        check_vma=False,
    )
```

```python
import functools
import math

import jax
import jax.numpy as jnp
from jax import lax
from jax.experimental import pallas as pl
from jax.experimental.pallas import tpu as pltpu
from jax.sharding import PartitionSpec as P

HEADS = 8
HEAD = 64
PATCH = 16
D = 512
COLS = 4096
PC = 256
LANES = 128
TILES = COLS // LANES
VPD = 8
DEVS = 8
OWN = PC // DEVS
BF = jnp.bfloat16
F32 = jnp.float32
NT = (((1,), (1,)), ((), ()))
SPARE = 8192


def three_parts(x):
    high = x.astype(BF)
    rest = x - high.astype(F32)
    middle = rest.astype(BF)
    return high, middle, (rest - middle.astype(F32)).astype(BF)


def relayout_group(rows, stage, edge_stage, out):
    for t in range(TILES):
        stage[t * 8 : t * 8 + 8, :] = rows[:, t * LANES : (t + 1) * LANES]
    skewed = [
        pltpu.roll(stage[pl.ds(r, TILES, stride=8), :].astype(BF), (16 * r + 8) % LANES, 1) for r in range(8)
    ]
    lane = lax.broadcasted_iota(jnp.int32, (TILES, LANES), 1)
    level = [skewed[(-k) % 8] for k in range(8)]
    for bit in (1, 2, 4):
        chosen = ((lane // 16) & bit) != 0
        level = [jnp.where(chosen, level[(k - bit) % 8], level[k]) for k in range(8)]
    for k in range(1, 8):
        out[k * TILES : (k + 1) * TILES, :] = pltpu.roll(level[k], (-16 * k) % LANES, 1)
    edge_stage[8 : 8 + TILES, :] = level[0].astype(F32)
    left = (lane % 16) < 8
    out[0:TILES, :] = jnp.where(left, edge_stage[7 : 7 + TILES, :].astype(BF), level[0])
    out[8 * TILES : 9 * TILES, :] = jnp.where(left, level[0], edge_stage[9 : 9 + TILES, :].astype(BF))


def permutation():
    row = lax.broadcasted_iota(jnp.int32, (PC, PC), 0)
    col = lax.broadcasted_iota(jnp.int32, (PC, PC), 1)
    same = ((row // 8) == (col % TILES)) & ((row % 8) == (col // TILES))
    return jnp.where(same, 1.0, 0.0).astype(BF)


def embed_kernel(edge, *refs):
    if edge:
        low_ref, high_ref, ext_hbm, *refs = refs
    else:
        query_hbm, key_hbm, value_hbm, *refs = refs
    px_hbm, w_hbm, cnt_hbm, ve_hbm, msg_ref, *refs = refs
    if not edge:
        ext_out, *refs = refs
    (px, w, ext, cnt_ref, ve_ref, a_even, a_odd, stage_even, stage_odd, edges, tok_even, tok_odd, bias_ref, off_ref,
     top_ref, tot_ref, acc_ref, px_sem, w_sem, sem, *more) = refs
    rows = (0, 3) if edge else (1, 2)
    starts = (0, 4) if edge else (0, 2)

    def px_copy(v):
        return pltpu.make_async_copy(px_hbm.at[v], px.at[v], px_sem.at[v])

    def w_copy(v):
        return pltpu.make_async_copy(w_hbm.at[v], w.at[v], w_sem.at[v])

    small = [(cnt_hbm, cnt_ref), (ve_hbm, ve_ref)]
    if edge:
        small.append((ext_hbm.at[0 : D + 32], ext))
    else:
        query_ref, key_ref, value_ref = more
        small += [(query_hbm, query_ref), (key_hbm, key_ref), (value_hbm, value_ref)]
    small = [pltpu.make_async_copy(src, dst, sem.at[n]) for n, (src, dst) in enumerate(small)]
    for copy in small[:2]:
        copy.start()
    px_copy(0).start()
    for copy in small[2:]:
        copy.start()
    w_copy(0).start()
    px_copy(1).start()

    def relayout(v, a_ref, stage):
        body = px[v].astype(F32)
        if edge:
            groups = [low_ref[v].astype(F32), body[0:8], body[8:16], body[16:24],
                      body[40:48], body[48:56], body[56:64], high_ref[v].astype(F32)]
        else:
            groups = [body[8 * n : 8 * n + 8] for n in range(1, 7)]
        for n, group in enumerate(groups):
            relayout_group(group, stage.at[n], edges.at[n], a_ref.at[n])

    def embed_tokens(v, a_ref, tok):
        a = jnp.concatenate(
            [
                jnp.concatenate([a_ref[start + g, b * TILES : b * TILES + PC, :] for g in range(4) for b in range(2)], 1)
                for start in starts
            ],
            0,
        )
        weight = jnp.concatenate(
            [w[v, 8 * g : 8 * g + 8, 16 * b : 16 * b + 16, :].reshape(LANES, D) for g in range(4) for b in range(2)], 0
        )
        tok[...] = (jnp.dot(a, weight, preferred_element_type=F32) + off_ref[v]).astype(BF)

    def attend(v, tok):
        both = lax.dot_general(ext[...], tok[...], NT, preferred_element_type=F32)
        scores = both[0:8] + both[8:16] + both[16:24] + bias_ref[v]
        old = top_ref[...]
        top = jnp.maximum(old, scores)
        decay = jnp.exp(old - top)
        fresh = jnp.exp(scores - top)
        top_ref[...] = top
        tot_ref[...] = tot_ref[...] * decay + fresh
        for h in range(HEADS):
            at = slice(h * HEAD, (h + 1) * HEAD)
            acc_ref[at, :] = acc_ref[at, :] * decay[h : h + 1] + both[32 + h * HEAD : 32 + (h + 1) * HEAD] * fresh[h : h + 1]

    edges[...] = jnp.zeros_like(edges)
    perm = permutation()
    small[0].wait()
    small[1].wait()
    valid = jnp.concatenate([cnt_ref[v].astype(F32) for v in range(VPD)], 0).astype(BF)
    bias = jnp.log((1.0 + jnp.dot(valid, perm, preferred_element_type=F32)) / (1.0 + PATCH * PATCH))
    offsets = ve_ref[...].astype(F32)
    for v in range(VPD):
        off_ref[v] = offsets[v : v + 1]
        bias_ref[v] = jnp.concatenate([bias[4 * v + row : 4 * v + row + 1] for row in rows], 1)
    top_ref[...] = jnp.full_like(top_ref, -1e30)
    tot_ref[...] = jnp.zeros_like(tot_ref)
    acc_ref[...] = jnp.zeros_like(acc_ref)
    px_copy(0).wait()
    w_copy(1).start()
    px_copy(2).start()
    relayout(0, a_even, stage_even)
    w_copy(2).start()
    px_copy(3).start()
    w_copy(0).wait()
    px_copy(1).wait()
    for copy in small[2:]:
        copy.wait()
    if not edge:
        head = lax.broadcasted_iota(jnp.int32, (HEADS, D), 0)
        col = lax.broadcasted_iota(jnp.int32, (HEADS, D), 1)
        spread = jnp.where(col // HEAD == head, jnp.broadcast_to(query_ref[...], (HEADS, D)), 0.0)
        parts = lax.dot_general(jnp.concatenate(three_parts(spread), 0), key_ref[...], NT, preferred_element_type=F32)
        kq = (parts[0:8] + parts[8:16] + parts[16:24]) / math.sqrt(HEAD)
        ext[32 : D + 32, :] = value_ref[...].T
        ext[0:32, :] = jnp.concatenate((*three_parts(kq), jnp.zeros((8, D), BF)), 0)
        ext_copy = pltpu.make_async_copy(ext, ext_out.at[0 : D + 32], sem.at[0])
        ext_copy.start()
    embed_tokens(0, a_even, tok_even)
    relayout(1, a_odd, stage_odd)

    def pair(step, _):
        odd = 2 * step + 1

        @pl.when(step < VPD // 2 - 2)
        def _():
            for v in (odd + 2, odd + 3):
                w_copy(v).start()
                px_copy(v + 1).start()

        @pl.when(step == VPD // 2 - 2)
        def _():
            w_copy(VPD - 1).start()

        for v in (odd, odd + 1):
            w_copy(v).wait()
            px_copy(v + 1).wait()
        embed_tokens(odd, a_odd, tok_odd)
        attend(odd - 1, tok_even)
        relayout(odd + 1, a_even, stage_even)
        embed_tokens(odd + 1, a_even, tok_even)
        attend(odd, tok_odd)
        relayout(odd + 2, a_odd, stage_odd)
        return 0

    lax.fori_loop(0, VPD // 2 - 1, pair, 0)
    w_copy(VPD - 1).wait()
    embed_tokens(VPD - 1, a_odd, tok_odd)
    attend(VPD - 2, tok_even)
    attend(VPD - 1, tok_odd)
    if not edge:
        ext_copy.wait()

    lane = lax.broadcasted_iota(jnp.int32, (24, LANES), 1)
    total = tot_ref[...]
    parts = jnp.concatenate(three_parts(top_ref[...] + jnp.log(total)), 0)
    sums = []
    for n in range(2):
        half = slice(n * PC, (n + 1) * PC)
        weighted = jnp.concatenate(
            [acc_ref[h * HEAD : (h + 1) * HEAD, half] / total[h : h + 1, half] for h in range(HEADS)], 0
        ).astype(BF)
        natural = lax.dot_general(perm, weighted, NT, preferred_element_type=F32).astype(BF)
        for d in range(DEVS):
            msg_ref[d, n * OWN : (n + 1) * OWN, :] = natural[d * OWN : (d + 1) * OWN]
        sums.append(lax.dot_general(parts[:, half], perm, NT, preferred_element_type=F32))
    for d in range(DEVS):
        spot = d * OWN // LANES * LANES
        picked = jnp.zeros((24, LANES), F32)
        for n in range(2):
            moved = pltpu.roll(sums[n][:, spot : spot + LANES], (n * OWN - d * OWN) % LANES, 1)
            picked = jnp.where(lane // OWN == n, moved, picked)
        wide = jnp.concatenate([picked[0:8], picked[8:16], picked[16:24], jnp.zeros((8, LANES), F32)], 1)
        msg_ref[d, 2 * OWN : 2 * OWN + 16, :] = jnp.concatenate([wide, jnp.zeros((8, D), F32)], 0).astype(BF)


def embed(edge, extras, pixels, weight, counts, var_embed):
    groups = 8 if edge else 6
    hbm = pl.BlockSpec(memory_space=pltpu.HBM)
    vmem = pl.BlockSpec(memory_space=pltpu.VMEM)
    out_shape = [jax.ShapeDtypeStruct((DEVS, 2 * OWN + 16, D), BF)]
    scratch = [
        pltpu.VMEM((VPD, 64, COLS), BF),
        pltpu.VMEM((VPD, 32, 32, D), BF),
        pltpu.VMEM((D + 32, D), BF),
        pltpu.VMEM((VPD, 4, PC), jnp.int32),
        pltpu.VMEM((VPD, D), BF),
        pltpu.VMEM((groups, PC + TILES, LANES), BF),
        pltpu.VMEM((groups, PC + TILES, LANES), BF),
        pltpu.VMEM((groups, TILES * 8, LANES), F32),
        pltpu.VMEM((groups, TILES * 8, LANES), F32),
        pltpu.VMEM((groups, TILES + 16, LANES), F32),
        pltpu.VMEM((D, D), BF),
        pltpu.VMEM((D, D), BF),
        pltpu.VMEM((VPD, 1, 2 * PC), F32),
        pltpu.VMEM((VPD, 1, D), F32),
        pltpu.VMEM((HEADS, 2 * PC), F32),
        pltpu.VMEM((HEADS, 2 * PC), F32),
        pltpu.VMEM((D, 2 * PC), F32),
        pltpu.SemaphoreType.DMA((VPD,)),
        pltpu.SemaphoreType.DMA((VPD,)),
        pltpu.SemaphoreType.DMA((5,)),
    ]
    if not edge:
        out_shape.append(jax.ShapeDtypeStruct((SPARE, D), BF))
        scratch += [pltpu.VMEM((1, D), F32), pltpu.VMEM((D, D), BF), pltpu.VMEM((D, D), BF)]
    return pl.pallas_call(
        functools.partial(embed_kernel, edge),
        in_specs=[vmem if edge else hbm] * 2 + [hbm] * 5,
        out_specs=[vmem, hbm][: len(out_shape)],
        out_shape=out_shape,
        scratch_shapes=scratch,
        compiler_params=pltpu.CompilerParams(vmem_limit_bytes=(48 if edge else 56) * 2**20),
        cost_estimate=pl.CostEstimate(flops=8 * 2 * 512 * (1024 + 512) * 512, bytes_accessed=13 * 2**20, transcendentals=0),
        name="embed_edge" if edge else "embed_inner",
    )(*extras, pixels, weight, counts, var_embed)


def finish_kernel(msg_ref, wo_ref, *refs):
    sums = []
    for s in range(DEVS):
        wide = msg_ref[s, 2 * OWN : 2 * OWN + 16, :].astype(F32)[0:8]
        sums.append(wide[:, 0:LANES] + wide[:, LANES : 2 * LANES] + wide[:, 2 * LANES : 3 * LANES])
    top = functools.reduce(jnp.maximum, sums)
    parts = [jnp.exp(x - top) for x in sums]
    scale = 1.0 / functools.reduce(jnp.add, parts)
    shares = []
    for part in parts:
        share = part * scale
        high = share.astype(BF).astype(F32)
        shares += [high, share - high]
    shares = jnp.concatenate(shares, 0).T[0 : 2 * OWN].astype(BF)
    row = lax.broadcasted_iota(jnp.int32, (LANES, D), 0)
    col = lax.broadcasted_iota(jnp.int32, (LANES, D), 1)
    spread = jnp.where((row < 16) & (col // HEAD == row % HEADS), 1.0, 0.0).astype(BF)
    turned = [pltpu.roll(shares, (-16 * s) % LANES, 1) if s else shares for s in range(DEVS)]
    wide = jnp.dot(jnp.concatenate(turned, 0), spread, preferred_element_type=F32)
    mixture = jnp.zeros((2 * OWN, D), F32)
    for s in range(DEVS):
        mixture = mixture + wide[s * 2 * OWN : (s + 1) * 2 * OWN] * msg_ref[s, 0 : 2 * OWN, :].astype(F32)
    result = jnp.dot(mixture.astype(BF), wo_ref[...], preferred_element_type=F32).astype(BF)
    *inner_ref, out_ref = refs
    if inner_ref:
        out_ref[0] = result[0:OWN]
        out_ref[1:3] = inner_ref[0][...]
        out_ref[3] = result[OWN : 2 * OWN]
    else:
        out_ref[0] = result[0:OWN]
        out_ref[1] = result[OWN : 2 * OWN]


def finish(msg, out_weight, *inner):
    return pl.pallas_call(
        finish_kernel,
        out_shape=jax.ShapeDtypeStruct((2 + 2 * len(inner), OWN, D), BF),
        compiler_params=pltpu.CompilerParams(vmem_limit_bytes=24 * 2**20),
        cost_estimate=pl.CostEstimate(flops=2 * 64 * 512 * 512, bytes_accessed=2**20, transcendentals=0),
        name="finish_edge" if inner else "finish_inner",
    )(msg, out_weight, *inner)


def exchange(msg):
    return lax.all_to_all(msg, "var", 0, 0)


def shards(pixels, counts, embed_weight, var_embed, query, key_weight, value_weight, out_weight):
    count = lax.axis_size("space")
    forward = [(i, i + 1) for i in range(count - 1)]
    low = lax.ppermute(pixels[:, 56:64], "space", forward)
    high = lax.ppermute(pixels[:, 0:8], "space", [(b, a) for a, b in forward])
    rest = (pixels, embed_weight, counts, var_embed)
    inner, ext = embed(False, (query.reshape(1, D), key_weight, value_weight), *rest)
    inner = exchange(inner)
    (outer,) = embed(True, (low, high, ext), *rest)
    outer = exchange(outer)
    return finish(outer, out_weight, finish(inner, out_weight))


def solution(mesh):
    return jax.shard_map(
        shards,
        mesh=mesh,
        in_specs=(
            P("var", "space", None),
            P("var", "space", None),
            P("var", None, None, None),
            P("var", None),
            P(),
            P(),
            P(),
            P(),
        ),
        out_specs=P("space", "var", None),
        check_vma=False,
    )
```

```python
import functools
import math

import jax
import jax.numpy as jnp
from jax import lax
from jax.experimental import pallas as pl
from jax.experimental.pallas import tpu as pltpu
from jax.sharding import PartitionSpec as P

HEADS = 8
HEAD = 64
PATCH = 16
D = 512
COLS = 4096
PC = 256
LANES = 128
TILES = COLS // LANES
VPD = 8
DEVS = 8
OWN = PC // DEVS
MESSAGE = 2 * OWN + 8
BF = jnp.bfloat16
F32 = jnp.float32
NT = (((1,), (1,)), ((), ()))
SPARE = 8192


def three_parts(x):
    high = x.astype(BF)
    rest = x - high.astype(F32)
    middle = rest.astype(BF)
    return high, middle, (rest - middle.astype(F32)).astype(BF)


def relayout_group(rows, stage, edge_stage, out):
    for t in range(TILES):
        stage[t * 8 : t * 8 + 8, :] = rows[:, t * LANES : (t + 1) * LANES]
    skewed = [
        pltpu.roll(stage[pl.ds(r, TILES, stride=8), :].astype(BF), (16 * r + 8) % LANES, 1) for r in range(8)
    ]
    lane = lax.broadcasted_iota(jnp.int32, (TILES, LANES), 1)
    level = [skewed[(-k) % 8] for k in range(8)]
    for bit in (1, 2, 4):
        chosen = ((lane // 16) & bit) != 0
        level = [jnp.where(chosen, level[(k - bit) % 8], level[k]) for k in range(8)]
    for k in range(1, 8):
        out[k * TILES : (k + 1) * TILES, :] = pltpu.roll(level[k], (-16 * k) % LANES, 1)
    edge_stage[8 : 8 + TILES, :] = level[0].astype(F32)
    left = (lane % 16) < 8
    out[0:TILES, :] = jnp.where(left, edge_stage[7 : 7 + TILES, :].astype(BF), level[0])
    out[8 * TILES : 9 * TILES, :] = jnp.where(left, level[0], edge_stage[9 : 9 + TILES, :].astype(BF))


def permutation():
    row = lax.broadcasted_iota(jnp.int32, (PC, PC), 0)
    col = lax.broadcasted_iota(jnp.int32, (PC, PC), 1)
    same = ((row // 8) == (col % TILES)) & ((row % 8) == (col // TILES))
    return jnp.where(same, 1.0, 0.0).astype(BF)


def embed_kernel(edge, *refs):
    if edge:
        low_ref, high_ref, ext_hbm, *refs = refs
    else:
        query_hbm, key_hbm, value_hbm, *refs = refs
    px_hbm, w_hbm, cnt_hbm, ve_hbm, msg_ref, *refs = refs
    if not edge:
        ext_out, *refs = refs
    (px, w, ext, cnt_ref, ve_ref, a_even, a_odd, stage_even, stage_odd, edges, tok_even, tok_odd, bias_ref, off_ref,
     top_ref, tot_ref, acc_ref, px_sem, w_sem, sem, *more) = refs
    rows = (0, 3) if edge else (1, 2)
    starts = (0, 4) if edge else (0, 2)

    def px_copy(v):
        return pltpu.make_async_copy(px_hbm.at[v], px.at[v], px_sem.at[v])

    def w_copy(v):
        return pltpu.make_async_copy(w_hbm.at[v], w.at[v], w_sem.at[v])

    small = [(cnt_hbm, cnt_ref), (ve_hbm, ve_ref)]
    if edge:
        small.append((ext_hbm.at[0 : D + 32], ext))
    else:
        query_ref, key_ref, value_ref = more
        small += [(query_hbm, query_ref), (key_hbm, key_ref), (value_hbm, value_ref)]
    small = [pltpu.make_async_copy(src, dst, sem.at[n]) for n, (src, dst) in enumerate(small)]
    for copy in small[:2]:
        copy.start()
    px_copy(0).start()
    for copy in small[2:]:
        copy.start()
    w_copy(0).start()
    px_copy(1).start()

    def relayout(v, a_ref, stage):
        body = px[v].astype(F32)
        if edge:
            groups = [low_ref[v].astype(F32), body[0:8], body[8:16], body[16:24],
                      body[40:48], body[48:56], body[56:64], high_ref[v].astype(F32)]
        else:
            groups = [body[8 * n : 8 * n + 8] for n in range(1, 7)]
        for n, group in enumerate(groups):
            relayout_group(group, stage.at[n], edges.at[n], a_ref.at[n])

    def embed_tokens(v, a_ref, tok):
        a = jnp.concatenate(
            [
                jnp.concatenate([a_ref[start + g, b * TILES : b * TILES + PC, :] for g in range(4) for b in range(2)], 1)
                for start in starts
            ],
            0,
        )
        weight = jnp.concatenate(
            [w[v, 8 * g : 8 * g + 8, 16 * b : 16 * b + 16, :].reshape(LANES, D) for g in range(4) for b in range(2)], 0
        )
        tok[...] = (jnp.dot(a, weight, preferred_element_type=F32) + off_ref[v]).astype(BF)

    def attend(v, tok):
        both = lax.dot_general(ext[...], tok[...], NT, preferred_element_type=F32)
        scores = both[0:8] + both[8:16] + both[16:24] + bias_ref[v]
        old = top_ref[...]
        top = jnp.maximum(old, scores)
        decay = jnp.exp(old - top)
        fresh = jnp.exp(scores - top)
        top_ref[...] = top
        tot_ref[...] = tot_ref[...] * decay + fresh
        for h in range(HEADS):
            at = slice(h * HEAD, (h + 1) * HEAD)
            acc_ref[at, :] = acc_ref[at, :] * decay[h : h + 1] + both[32 + h * HEAD : 32 + (h + 1) * HEAD] * fresh[h : h + 1]

    edges[...] = jnp.zeros_like(edges)
    perm = permutation()
    small[0].wait()
    small[1].wait()
    valid = jnp.concatenate([cnt_ref[v].astype(F32) for v in range(VPD)], 0).astype(BF)
    bias = jnp.log((1.0 + jnp.dot(valid, perm, preferred_element_type=F32)) / (1.0 + PATCH * PATCH))
    offsets = ve_ref[...].astype(F32)
    for v in range(VPD):
        off_ref[v] = offsets[v : v + 1]
        bias_ref[v] = jnp.concatenate([bias[4 * v + row : 4 * v + row + 1] for row in rows], 1)
    top_ref[...] = jnp.full_like(top_ref, -1e30)
    tot_ref[...] = jnp.zeros_like(tot_ref)
    acc_ref[...] = jnp.zeros_like(acc_ref)
    px_copy(0).wait()
    w_copy(1).start()
    px_copy(2).start()
    relayout(0, a_even, stage_even)
    w_copy(2).start()
    px_copy(3).start()
    w_copy(0).wait()
    px_copy(1).wait()
    for copy in small[2:]:
        copy.wait()
    if not edge:
        head = lax.broadcasted_iota(jnp.int32, (HEADS, D), 0)
        col = lax.broadcasted_iota(jnp.int32, (HEADS, D), 1)
        spread = jnp.where(col // HEAD == head, jnp.broadcast_to(query_ref[...], (HEADS, D)), 0.0)
        parts = lax.dot_general(jnp.concatenate(three_parts(spread), 0), key_ref[...], NT, preferred_element_type=F32)
        kq = (parts[0:8] + parts[8:16] + parts[16:24]) / math.sqrt(HEAD)
        ext[32 : D + 32, :] = value_ref[...].T
        ext[0:32, :] = jnp.concatenate((*three_parts(kq), jnp.zeros((8, D), BF)), 0)
        ext_copy = pltpu.make_async_copy(ext, ext_out.at[0 : D + 32], sem.at[0])
        ext_copy.start()
    embed_tokens(0, a_even, tok_even)
    relayout(1, a_odd, stage_odd)

    def pair(step, _):
        odd = 2 * step + 1

        @pl.when(step < VPD // 2 - 2)
        def _():
            for v in (odd + 2, odd + 3):
                w_copy(v).start()
                px_copy(v + 1).start()

        @pl.when(step == VPD // 2 - 2)
        def _():
            w_copy(VPD - 1).start()

        for v in (odd, odd + 1):
            w_copy(v).wait()
            px_copy(v + 1).wait()
        embed_tokens(odd, a_odd, tok_odd)
        attend(odd - 1, tok_even)
        relayout(odd + 1, a_even, stage_even)
        embed_tokens(odd + 1, a_even, tok_even)
        attend(odd, tok_odd)
        relayout(odd + 2, a_odd, stage_odd)
        return 0

    lax.fori_loop(0, VPD // 2 - 1, pair, 0)
    w_copy(VPD - 1).wait()
    embed_tokens(VPD - 1, a_odd, tok_odd)
    attend(VPD - 2, tok_even)
    attend(VPD - 1, tok_odd)
    if not edge:
        ext_copy.wait()

    lane = lax.broadcasted_iota(jnp.int32, (24, LANES), 1)
    total = tot_ref[...]
    parts = jnp.concatenate(three_parts(top_ref[...] + jnp.log(total)), 0)
    sums = []
    for n in range(2):
        half = slice(n * PC, (n + 1) * PC)
        weighted = jnp.concatenate(
            [acc_ref[h * HEAD : (h + 1) * HEAD, half] / total[h : h + 1, half] for h in range(HEADS)], 0
        ).astype(BF)
        natural = lax.dot_general(perm, weighted, NT, preferred_element_type=F32).astype(BF)
        for d in range(DEVS):
            msg_ref[d, n * OWN : (n + 1) * OWN, :] = natural[d * OWN : (d + 1) * OWN]
        sums.append(lax.dot_general(parts[:, half], perm, NT, preferred_element_type=F32))
    base = 2 * OWN if edge else 0
    for d in range(DEVS):
        spot = d * OWN // LANES * LANES
        picked = jnp.zeros((24, LANES), F32)
        for n in range(2):
            moved = pltpu.roll(sums[n][:, spot : spot + LANES], (base + n * OWN - d * OWN) % LANES, 1)
            picked = jnp.where(lane // OWN == base // OWN + n, moved, picked)
        wide = jnp.concatenate([picked[0:8], picked[8:16], picked[16:24], jnp.zeros((8, LANES), F32)], 1)
        msg_ref[d, 2 * OWN : MESSAGE, :] = wide.astype(BF)


def embed(edge, extras, pixels, weight, counts, var_embed):
    groups = 8 if edge else 6
    hbm = pl.BlockSpec(memory_space=pltpu.HBM)
    vmem = pl.BlockSpec(memory_space=pltpu.VMEM)
    out_shape = [jax.ShapeDtypeStruct((DEVS, MESSAGE, D), BF)]
    scratch = [
        pltpu.VMEM((VPD, 64, COLS), BF),
        pltpu.VMEM((VPD, 32, 32, D), BF),
        pltpu.VMEM((D + 32, D), BF),
        pltpu.VMEM((VPD, 4, PC), jnp.int32),
        pltpu.VMEM((VPD, D), BF),
        pltpu.VMEM((groups, PC + TILES, LANES), BF),
        pltpu.VMEM((groups, PC + TILES, LANES), BF),
        pltpu.VMEM((groups, TILES * 8, LANES), F32),
        pltpu.VMEM((groups, TILES * 8, LANES), F32),
        pltpu.VMEM((groups, TILES + 16, LANES), F32),
        pltpu.VMEM((D, D), BF),
        pltpu.VMEM((D, D), BF),
        pltpu.VMEM((VPD, 1, 2 * PC), F32),
        pltpu.VMEM((VPD, 1, D), F32),
        pltpu.VMEM((HEADS, 2 * PC), F32),
        pltpu.VMEM((HEADS, 2 * PC), F32),
        pltpu.VMEM((D, 2 * PC), F32),
        pltpu.SemaphoreType.DMA((VPD,)),
        pltpu.SemaphoreType.DMA((VPD,)),
        pltpu.SemaphoreType.DMA((5,)),
    ]
    if not edge:
        out_shape.append(jax.ShapeDtypeStruct((SPARE, D), BF))
        scratch += [pltpu.VMEM((1, D), F32), pltpu.VMEM((D, D), BF), pltpu.VMEM((D, D), BF)]
    return pl.pallas_call(
        functools.partial(embed_kernel, edge),
        in_specs=[vmem if edge else hbm] * 2 + [hbm] * 5,
        out_specs=[vmem, hbm][: len(out_shape)],
        out_shape=out_shape,
        scratch_shapes=scratch,
        compiler_params=pltpu.CompilerParams(vmem_limit_bytes=(52 if edge else 56) * 2**20),
        cost_estimate=pl.CostEstimate(flops=8 * 2 * 512 * (1024 + 512) * 512, bytes_accessed=13 * 2**20, transcendentals=0),
        name="embed_edge" if edge else "embed_inner",
    )(*extras, pixels, weight, counts, var_embed)


def finish_kernel(inner_ref, outer_ref, wo_ref, out_ref):
    lane = lax.broadcasted_iota(jnp.int32, (HEADS, LANES), 1)
    sums = []
    for s in range(DEVS):
        a = inner_ref[s, 2 * OWN : MESSAGE, :].astype(F32)
        b = outer_ref[s, 2 * OWN : MESSAGE, :].astype(F32)
        a = a[:, 0:LANES] + a[:, LANES : 2 * LANES] + a[:, 2 * LANES : 3 * LANES]
        b = b[:, 0:LANES] + b[:, LANES : 2 * LANES] + b[:, 2 * LANES : 3 * LANES]
        sums.append(jnp.where(lane < 2 * OWN, a, b))
    top = functools.reduce(jnp.maximum, sums)
    parts = [jnp.exp(x - top) for x in sums]
    scale = 1.0 / functools.reduce(jnp.add, parts)
    shares = []
    for part in parts:
        share = part * scale
        high = share.astype(BF).astype(F32)
        shares += [high, share - high]
    shares = jnp.concatenate(shares, 0).T.astype(BF)
    row = lax.broadcasted_iota(jnp.int32, (LANES, D), 0)
    col = lax.broadcasted_iota(jnp.int32, (LANES, D), 1)
    spread = jnp.where((row < 16) & (col // HEAD == row % HEADS), 1.0, 0.0).astype(BF)
    turned = [pltpu.roll(shares, (-16 * s) % LANES, 1) if s else shares for s in range(DEVS)]
    wide = jnp.dot(jnp.concatenate(turned, 0), spread, preferred_element_type=F32)
    mixture = jnp.zeros((LANES, D), F32)
    for s in range(DEVS):
        values = jnp.concatenate([inner_ref[s, 0 : 2 * OWN, :], outer_ref[s, 0 : 2 * OWN, :]], 0)
        mixture = mixture + wide[s * LANES : (s + 1) * LANES] * values.astype(F32)
    result = jnp.dot(mixture.astype(BF), wo_ref[...], preferred_element_type=F32).astype(BF)
    for n, row in enumerate((1, 2, 0, 3)):
        out_ref[row] = result[n * OWN : (n + 1) * OWN]


def finish(inner, outer, out_weight):
    return pl.pallas_call(
        finish_kernel,
        out_shape=jax.ShapeDtypeStruct((4, OWN, D), BF),
        compiler_params=pltpu.CompilerParams(vmem_limit_bytes=24 * 2**20),
        cost_estimate=pl.CostEstimate(flops=2 * 128 * 512 * 512, bytes_accessed=2**21, transcendentals=0),
        name="finish",
    )(inner, outer, out_weight)


def exchange(msg):
    return lax.all_to_all(msg, "var", 0, 0)


def shards(pixels, counts, embed_weight, var_embed, query, key_weight, value_weight, out_weight):
    count = lax.axis_size("space")
    forward = [(i, i + 1) for i in range(count - 1)]
    low = lax.ppermute(pixels[:, 56:64], "space", forward)
    high = lax.ppermute(pixels[:, 0:8], "space", [(b, a) for a, b in forward])
    rest = (pixels, embed_weight, counts, var_embed)
    inner, ext = embed(False, (query.reshape(1, D), key_weight, value_weight), *rest)
    inner = exchange(inner)
    (outer,) = embed(True, (low, high, ext), *rest)
    outer = exchange(outer)
    return finish(inner, outer, out_weight)


def solution(mesh):
    return jax.shard_map(
        shards,
        mesh=mesh,
        in_specs=(
            P("var", "space", None),
            P("var", "space", None),
            P("var", None, None, None),
            P("var", None),
            P(),
            P(),
            P(),
            P(),
        ),
        out_specs=P("space", "var", None),
        check_vma=False,
    )
```

```python
import functools
import math

import jax
import jax.numpy as jnp
from jax import lax
from jax.experimental import pallas as pl
from jax.experimental.pallas import tpu as pltpu
from jax.sharding import PartitionSpec as P

HEADS = 8
HEAD = 64
PATCH = 16
D = 512
COLS = 4096
PC = 256
LANES = 128
TILES = COLS // LANES
VPD = 8
DEVS = 8
OWN = PC // DEVS
MESSAGE = 2 * OWN + 8
BF = jnp.bfloat16
F32 = jnp.float32
NT = (((1,), (1,)), ((), ()))
SPARE = 8192


def three_parts(x):
    high = x.astype(BF)
    rest = x - high.astype(F32)
    middle = rest.astype(BF)
    return high, middle, (rest - middle.astype(F32)).astype(BF)


def relayout_group(rows, stage, edge_stage, out):
    for t in range(TILES):
        stage[t * 8 : t * 8 + 8, :] = rows[:, t * LANES : (t + 1) * LANES]
    skewed = [
        pltpu.roll(stage[pl.ds(r, TILES, stride=8), :].astype(BF), (16 * r + 8) % LANES, 1) for r in range(8)
    ]
    lane = lax.broadcasted_iota(jnp.int32, (TILES, LANES), 1)
    level = [skewed[(-k) % 8] for k in range(8)]
    for bit in (1, 2, 4):
        chosen = ((lane // 16) & bit) != 0
        level = [jnp.where(chosen, level[(k - bit) % 8], level[k]) for k in range(8)]
    for k in range(1, 8):
        out[k * TILES : (k + 1) * TILES, :] = pltpu.roll(level[k], (-16 * k) % LANES, 1)
    edge_stage[8 : 8 + TILES, :] = level[0].astype(F32)
    left = (lane % 16) < 8
    out[0:TILES, :] = jnp.where(left, edge_stage[7 : 7 + TILES, :].astype(BF), level[0])
    out[8 * TILES : 9 * TILES, :] = jnp.where(left, level[0], edge_stage[9 : 9 + TILES, :].astype(BF))


def permutation():
    row = lax.broadcasted_iota(jnp.int32, (PC, PC), 0)
    col = lax.broadcasted_iota(jnp.int32, (PC, PC), 1)
    same = ((row // 8) == (col % TILES)) & ((row % 8) == (col // TILES))
    return jnp.where(same, 1.0, 0.0).astype(BF)


def embed_kernel(edge, *refs):
    if edge:
        far_ref, near_ref, ext_hbm, *refs = refs
        odd_tile = lax.rem(lax.axis_index("space"), 2) == 1
    else:
        query_hbm, key_hbm, value_hbm, *refs = refs
    px_hbm, w_hbm, cnt_hbm, ve_hbm, msg_ref, *refs = refs
    if not edge:
        ext_out, *refs = refs
    (px, w, ext, cnt_ref, ve_ref, a_even, a_odd, stage_even, stage_odd, edges, tok_even, tok_odd, bias_ref, off_ref,
     top_ref, tot_ref, acc_ref, px_sem, w_sem, sem, *more) = refs
    rows = (0, 3) if edge else (1, 2)
    starts = (0, 4) if edge else (0, 2)

    def px_copy(v):
        return pltpu.make_async_copy(px_hbm.at[v], px.at[v], px_sem.at[v])

    def w_copy(v):
        return pltpu.make_async_copy(w_hbm.at[v], w.at[v], w_sem.at[v])

    small = [(cnt_hbm, cnt_ref), (ve_hbm, ve_ref)]
    if edge:
        small.append((ext_hbm.at[0 : D + 32], ext))
    else:
        query_ref, key_ref, value_ref = more
        small += [(query_hbm, query_ref), (key_hbm, key_ref), (value_hbm, value_ref)]
    small = [pltpu.make_async_copy(src, dst, sem.at[n]) for n, (src, dst) in enumerate(small)]
    for copy in small[:2]:
        copy.start()
    px_copy(0).start()
    for copy in small[2:]:
        copy.start()
    w_copy(0).start()
    px_copy(1).start()

    def relayout(v, a_ref, stage):
        body = px[v].astype(F32)
        if edge:
            far, near = far_ref[v].astype(F32), near_ref[v].astype(F32)
            groups = [jnp.where(odd_tile, near, far), body[0:8], body[8:16], body[16:24],
                      body[40:48], body[48:56], body[56:64], jnp.where(odd_tile, far, near)]
        else:
            groups = [body[8 * n : 8 * n + 8] for n in range(1, 7)]
        for n, group in enumerate(groups):
            relayout_group(group, stage.at[n], edges.at[n], a_ref.at[n])

    def embed_tokens(v, a_ref, tok):
        a = jnp.concatenate(
            [
                jnp.concatenate([a_ref[start + g, b * TILES : b * TILES + PC, :] for g in range(4) for b in range(2)], 1)
                for start in starts
            ],
            0,
        )
        weight = jnp.concatenate(
            [w[v, 8 * g : 8 * g + 8, 16 * b : 16 * b + 16, :].reshape(LANES, D) for g in range(4) for b in range(2)], 0
        )
        tok[...] = (jnp.dot(a, weight, preferred_element_type=F32) + off_ref[v]).astype(BF)

    def attend(v, tok):
        both = lax.dot_general(ext[...], tok[...], NT, preferred_element_type=F32)
        scores = both[0:8] + both[8:16] + both[16:24] + bias_ref[v]
        old = top_ref[...]
        top = jnp.maximum(old, scores)
        decay = jnp.exp(old - top)
        fresh = jnp.exp(scores - top)
        top_ref[...] = top
        tot_ref[...] = tot_ref[...] * decay + fresh
        for h in range(HEADS):
            at = slice(h * HEAD, (h + 1) * HEAD)
            acc_ref[at, :] = acc_ref[at, :] * decay[h : h + 1] + both[32 + h * HEAD : 32 + (h + 1) * HEAD] * fresh[h : h + 1]

    edges[...] = jnp.zeros_like(edges)
    perm = permutation()
    small[0].wait()
    small[1].wait()
    valid = jnp.concatenate([cnt_ref[v].astype(F32) for v in range(VPD)], 0).astype(BF)
    bias = jnp.log((1.0 + jnp.dot(valid, perm, preferred_element_type=F32)) / (1.0 + PATCH * PATCH))
    offsets = ve_ref[...].astype(F32)
    for v in range(VPD):
        off_ref[v] = offsets[v : v + 1]
        bias_ref[v] = jnp.concatenate([bias[4 * v + row : 4 * v + row + 1] for row in rows], 1)
    top_ref[...] = jnp.full_like(top_ref, -1e30)
    tot_ref[...] = jnp.zeros_like(tot_ref)
    acc_ref[...] = jnp.zeros_like(acc_ref)
    px_copy(0).wait()
    w_copy(1).start()
    px_copy(2).start()
    relayout(0, a_even, stage_even)
    w_copy(2).start()
    px_copy(3).start()
    w_copy(0).wait()
    px_copy(1).wait()
    for copy in small[2:]:
        copy.wait()
    if not edge:
        head = lax.broadcasted_iota(jnp.int32, (HEADS, D), 0)
        col = lax.broadcasted_iota(jnp.int32, (HEADS, D), 1)
        spread = jnp.where(col // HEAD == head, jnp.broadcast_to(query_ref[...], (HEADS, D)), 0.0)
        parts = lax.dot_general(jnp.concatenate(three_parts(spread), 0), key_ref[...], NT, preferred_element_type=F32)
        kq = (parts[0:8] + parts[8:16] + parts[16:24]) / math.sqrt(HEAD)
        ext[32 : D + 32, :] = value_ref[...].T
        ext[0:32, :] = jnp.concatenate((*three_parts(kq), jnp.zeros((8, D), BF)), 0)
        ext_copy = pltpu.make_async_copy(ext, ext_out.at[0 : D + 32], sem.at[0])
        ext_copy.start()
    embed_tokens(0, a_even, tok_even)
    relayout(1, a_odd, stage_odd)

    def pair(step, _):
        odd = 2 * step + 1

        @pl.when(step < VPD // 2 - 2)
        def _():
            for v in (odd + 2, odd + 3):
                w_copy(v).start()
                px_copy(v + 1).start()

        @pl.when(step == VPD // 2 - 2)
        def _():
            w_copy(VPD - 1).start()

        for v in (odd, odd + 1):
            w_copy(v).wait()
            px_copy(v + 1).wait()
        embed_tokens(odd, a_odd, tok_odd)
        attend(odd - 1, tok_even)
        relayout(odd + 1, a_even, stage_even)
        embed_tokens(odd + 1, a_even, tok_even)
        attend(odd, tok_odd)
        relayout(odd + 2, a_odd, stage_odd)
        return 0

    lax.fori_loop(0, VPD // 2 - 1, pair, 0)
    w_copy(VPD - 1).wait()
    embed_tokens(VPD - 1, a_odd, tok_odd)
    attend(VPD - 2, tok_even)
    attend(VPD - 1, tok_odd)
    if not edge:
        ext_copy.wait()

    lane = lax.broadcasted_iota(jnp.int32, (24, LANES), 1)
    total = tot_ref[...]
    parts = jnp.concatenate(three_parts(top_ref[...] + jnp.log(total)), 0)
    sums = []
    for n in range(2):
        half = slice(n * PC, (n + 1) * PC)
        weighted = jnp.concatenate(
            [acc_ref[h * HEAD : (h + 1) * HEAD, half] / total[h : h + 1, half] for h in range(HEADS)], 0
        ).astype(BF)
        natural = lax.dot_general(perm, weighted, NT, preferred_element_type=F32).astype(BF)
        for d in range(DEVS):
            msg_ref[d, n * OWN : (n + 1) * OWN, :] = natural[d * OWN : (d + 1) * OWN]
        sums.append(lax.dot_general(parts[:, half], perm, NT, preferred_element_type=F32))
    base = 2 * OWN if edge else 0
    for d in range(DEVS):
        spot = d * OWN // LANES * LANES
        picked = jnp.zeros((24, LANES), F32)
        for n in range(2):
            moved = pltpu.roll(sums[n][:, spot : spot + LANES], (base + n * OWN - d * OWN) % LANES, 1)
            picked = jnp.where(lane // OWN == base // OWN + n, moved, picked)
        wide = jnp.concatenate([picked[0:8], picked[8:16], picked[16:24], jnp.zeros((8, LANES), F32)], 1)
        msg_ref[d, 2 * OWN : MESSAGE, :] = wide.astype(BF)


def embed(edge, extras, pixels, weight, counts, var_embed):
    groups = 8 if edge else 6
    hbm = pl.BlockSpec(memory_space=pltpu.HBM)
    vmem = pl.BlockSpec(memory_space=pltpu.VMEM)
    out_shape = [jax.ShapeDtypeStruct((DEVS, MESSAGE, D), BF)]
    scratch = [
        pltpu.VMEM((VPD, 64, COLS), BF),
        pltpu.VMEM((VPD, 32, 32, D), BF),
        pltpu.VMEM((D + 32, D), BF),
        pltpu.VMEM((VPD, 4, PC), jnp.int32),
        pltpu.VMEM((VPD, D), BF),
        pltpu.VMEM((groups, PC + TILES, LANES), BF),
        pltpu.VMEM((groups, PC + TILES, LANES), BF),
        pltpu.VMEM((groups, TILES * 8, LANES), F32),
        pltpu.VMEM((groups, TILES * 8, LANES), F32),
        pltpu.VMEM((groups, TILES + 16, LANES), F32),
        pltpu.VMEM((D, D), BF),
        pltpu.VMEM((D, D), BF),
        pltpu.VMEM((VPD, 1, 2 * PC), F32),
        pltpu.VMEM((VPD, 1, D), F32),
        pltpu.VMEM((HEADS, 2 * PC), F32),
        pltpu.VMEM((HEADS, 2 * PC), F32),
        pltpu.VMEM((D, 2 * PC), F32),
        pltpu.SemaphoreType.DMA((VPD,)),
        pltpu.SemaphoreType.DMA((VPD,)),
        pltpu.SemaphoreType.DMA((5,)),
    ]
    if not edge:
        out_shape.append(jax.ShapeDtypeStruct((SPARE, D), BF))
        scratch += [pltpu.VMEM((1, D), F32), pltpu.VMEM((D, D), BF), pltpu.VMEM((D, D), BF)]
    return pl.pallas_call(
        functools.partial(embed_kernel, edge),
        in_specs=[vmem if edge else hbm] * 2 + [hbm] * 5,
        out_specs=[vmem, hbm][: len(out_shape)],
        out_shape=out_shape,
        scratch_shapes=scratch,
        compiler_params=pltpu.CompilerParams(vmem_limit_bytes=(52 if edge else 56) * 2**20),
        cost_estimate=pl.CostEstimate(flops=8 * 2 * 512 * (1024 + 512) * 512, bytes_accessed=13 * 2**20, transcendentals=0),
        name="embed_edge" if edge else "embed_inner",
    )(*extras, pixels, weight, counts, var_embed)


def finish_kernel(inner_ref, outer_ref, wo_ref, out_ref):
    lane = lax.broadcasted_iota(jnp.int32, (HEADS, LANES), 1)
    sums = []
    for s in range(DEVS):
        a = inner_ref[s, 2 * OWN : MESSAGE, :].astype(F32)
        b = outer_ref[s, 2 * OWN : MESSAGE, :].astype(F32)
        a = a[:, 0:LANES] + a[:, LANES : 2 * LANES] + a[:, 2 * LANES : 3 * LANES]
        b = b[:, 0:LANES] + b[:, LANES : 2 * LANES] + b[:, 2 * LANES : 3 * LANES]
        sums.append(jnp.where(lane < 2 * OWN, a, b))
    top = functools.reduce(jnp.maximum, sums)
    parts = [jnp.exp(x - top) for x in sums]
    scale = 1.0 / functools.reduce(jnp.add, parts)
    shares = []
    for part in parts:
        share = part * scale
        high = share.astype(BF).astype(F32)
        shares += [high, share - high]
    shares = jnp.concatenate(shares, 0).T.astype(BF)
    row = lax.broadcasted_iota(jnp.int32, (LANES, D), 0)
    col = lax.broadcasted_iota(jnp.int32, (LANES, D), 1)
    spread = jnp.where((row < 16) & (col // HEAD == row % HEADS), 1.0, 0.0).astype(BF)
    turned = [pltpu.roll(shares, (-16 * s) % LANES, 1) if s else shares for s in range(DEVS)]
    wide = jnp.dot(jnp.concatenate(turned, 0), spread, preferred_element_type=F32)
    mixture = jnp.zeros((LANES, D), F32)
    for s in range(DEVS):
        values = jnp.concatenate([inner_ref[s, 0 : 2 * OWN, :], outer_ref[s, 0 : 2 * OWN, :]], 0)
        mixture = mixture + wide[s * LANES : (s + 1) * LANES] * values.astype(F32)
    result = jnp.dot(mixture.astype(BF), wo_ref[...], preferred_element_type=F32).astype(BF)
    for n, row in enumerate((1, 2, 0, 3)):
        out_ref[row] = result[n * OWN : (n + 1) * OWN]


def finish(inner, outer, out_weight):
    return pl.pallas_call(
        finish_kernel,
        out_shape=jax.ShapeDtypeStruct((4, OWN, D), BF),
        compiler_params=pltpu.CompilerParams(vmem_limit_bytes=24 * 2**20),
        cost_estimate=pl.CostEstimate(flops=2 * 128 * 512 * 512, bytes_accessed=2**21, transcendentals=0),
        name="finish",
    )(inner, outer, out_weight)


def exchange(msg):
    return lax.all_to_all(msg, "var", 0, 0)


def shards(pixels, counts, embed_weight, var_embed, query, key_weight, value_weight, out_weight):
    count = lax.axis_size("space")
    odd = lax.rem(lax.axis_index("space"), 2)
    far_pairs = [(i, i + 1) for i in range(1, count - 1, 2)]
    near_pairs = [(i, i + 1) for i in range(0, count - 1, 2)]
    both_ways = lambda pairs: pairs + [(b, a) for a, b in pairs]
    reach = PATCH // 2
    last = pixels.shape[1] - reach
    far = lax.ppermute(lax.dynamic_slice_in_dim(pixels, odd * last, reach, 1), "space", both_ways(far_pairs))
    near = lax.ppermute(lax.dynamic_slice_in_dim(pixels, (1 - odd) * last, reach, 1), "space", both_ways(near_pairs))
    rest = (pixels, embed_weight, counts, var_embed)
    inner, ext = embed(False, (query.reshape(1, D), key_weight, value_weight), *rest)
    inner = exchange(inner)
    (outer,) = embed(True, (far, near, ext), *rest)
    outer = exchange(outer)
    return finish(inner, outer, out_weight)


def solution(mesh):
    return jax.shard_map(
        shards,
        mesh=mesh,
        in_specs=(
            P("var", "space", None),
            P("var", "space", None),
            P("var", None, None, None),
            P("var", None),
            P(),
            P(),
            P(),
            P(),
        ),
        out_specs=P("space", "var", None),
        check_vma=False,
    )
```

```python
import functools
import math

import jax
import jax.numpy as jnp
from jax import lax
from jax.experimental import pallas as pl
from jax.experimental.pallas import tpu as pltpu
from jax.sharding import PartitionSpec as P

HEADS = 8
HEAD = 64
PATCH = 16
D = 512
COLS = 4096
PC = 256
LANES = 128
TILES = COLS // LANES
VPD = 8
DEVS = 8
OWN = PC // DEVS
MESSAGE = 2 * OWN + 8
BF = jnp.bfloat16
F32 = jnp.float32
NT = (((1,), (1,)), ((), ()))
SPARE = 8192


def three_parts(x):
    high = x.astype(BF)
    rest = x - high.astype(F32)
    middle = rest.astype(BF)
    return high, middle, (rest - middle.astype(F32)).astype(BF)


def relayout_group(rows, stage, edge_stage, out):
    for t in range(TILES):
        stage[t * 8 : t * 8 + 8, :] = rows[:, t * LANES : (t + 1) * LANES]
    skewed = [
        pltpu.roll(stage[pl.ds(r, TILES, stride=8), :].astype(BF), (16 * r + 8) % LANES, 1) for r in range(8)
    ]
    lane = lax.broadcasted_iota(jnp.int32, (TILES, LANES), 1)
    level = [skewed[(-k) % 8] for k in range(8)]
    for bit in (1, 2, 4):
        chosen = ((lane // 16) & bit) != 0
        level = [jnp.where(chosen, level[(k - bit) % 8], level[k]) for k in range(8)]
    for k in range(1, 8):
        out[k * TILES : (k + 1) * TILES, :] = pltpu.roll(level[k], (-16 * k) % LANES, 1)
    edge_stage[8 : 8 + TILES, :] = level[0].astype(F32)
    left = (lane % 16) < 8
    out[0:TILES, :] = jnp.where(left, edge_stage[7 : 7 + TILES, :].astype(BF), level[0])
    out[8 * TILES : 9 * TILES, :] = jnp.where(left, level[0], edge_stage[9 : 9 + TILES, :].astype(BF))


def permutation():
    row = lax.broadcasted_iota(jnp.int32, (PC, PC), 0)
    col = lax.broadcasted_iota(jnp.int32, (PC, PC), 1)
    same = ((row // 8) == (col % TILES)) & ((row % 8) == (col // TILES))
    return jnp.where(same, 1.0, 0.0).astype(BF)


def embed_kernel(edge, *refs):
    if edge:
        far_ref, near_ref, ext_hbm, *refs = refs
        odd_tile = lax.rem(lax.axis_index("space"), 2) == 1
    else:
        query_hbm, key_hbm, value_hbm, *refs = refs
    px_hbm, w_hbm, cnt_hbm, ve_hbm, msg_ref, *refs = refs
    if not edge:
        ext_out, *refs = refs
    (px, w, ext, cnt_ref, ve_ref, a_even, a_odd, stage_even, stage_odd, edges, tok_even, tok_odd, bias_ref, off_ref,
     top_ref, tot_ref, acc_ref, px_sem, w_sem, sem, *more) = refs
    rows = (0, 3) if edge else (1, 2)
    starts = (0, 4) if edge else (0, 2)

    def px_copy(v):
        return pltpu.make_async_copy(px_hbm.at[v], px.at[v], px_sem.at[v])

    def w_copy(v):
        return pltpu.make_async_copy(w_hbm.at[v], w.at[v], w_sem.at[v])

    small = [(cnt_hbm, cnt_ref), (ve_hbm, ve_ref)]
    if edge:
        small.append((ext_hbm.at[0 : D + 32], ext))
    else:
        query_ref, key_ref, value_ref = more
        small += [(query_hbm, query_ref), (key_hbm, key_ref), (value_hbm, value_ref)]
    small = [pltpu.make_async_copy(src, dst, sem.at[n]) for n, (src, dst) in enumerate(small)]
    px_copy(0).start()
    for copy in small:
        copy.start()
    w_copy(0).start()
    px_copy(1).start()

    def relayout(v, a_ref, stage):
        body = px[v].astype(F32)
        if edge:
            far, near = far_ref[v].astype(F32), near_ref[v].astype(F32)
            groups = [jnp.where(odd_tile, near, far), body[0:8], body[8:16], body[16:24],
                      body[40:48], body[48:56], body[56:64], jnp.where(odd_tile, far, near)]
        else:
            groups = [body[8 * n : 8 * n + 8] for n in range(1, 7)]
        for n, group in enumerate(groups):
            relayout_group(group, stage.at[n], edges.at[n], a_ref.at[n])

    def embed_tokens(v, a_ref, tok):
        a = jnp.concatenate(
            [
                jnp.concatenate([a_ref[start + g, b * TILES : b * TILES + PC, :] for g in range(4) for b in range(2)], 1)
                for start in starts
            ],
            0,
        )
        weight = jnp.concatenate(
            [w[v, 8 * g : 8 * g + 8, 16 * b : 16 * b + 16, :].reshape(LANES, D) for g in range(4) for b in range(2)], 0
        )
        tok[...] = (jnp.dot(a, weight, preferred_element_type=F32) + off_ref[v]).astype(BF)

    def attend(v, tok):
        both = lax.dot_general(ext[...], tok[...], NT, preferred_element_type=F32)
        scores = both[0:8] + both[8:16] + both[16:24] + bias_ref[v]
        old = top_ref[...]
        top = jnp.maximum(old, scores)
        decay = jnp.exp(old - top)
        fresh = jnp.exp(scores - top)
        top_ref[...] = top
        tot_ref[...] = tot_ref[...] * decay + fresh
        for h in range(HEADS):
            at = slice(h * HEAD, (h + 1) * HEAD)
            acc_ref[at, :] = acc_ref[at, :] * decay[h : h + 1] + both[32 + h * HEAD : 32 + (h + 1) * HEAD] * fresh[h : h + 1]

    edges[...] = jnp.zeros_like(edges)
    perm = permutation()
    top_ref[...] = jnp.full_like(top_ref, -1e30)
    tot_ref[...] = jnp.zeros_like(tot_ref)
    acc_ref[...] = jnp.zeros_like(acc_ref)
    px_copy(0).wait()
    w_copy(1).start()
    px_copy(2).start()
    relayout(0, a_even, stage_even)
    w_copy(2).start()
    px_copy(3).start()
    small[0].wait()
    small[1].wait()
    valid = jnp.concatenate([cnt_ref[v].astype(F32) for v in range(VPD)], 0).astype(BF)
    bias = jnp.log((1.0 + jnp.dot(valid, perm, preferred_element_type=F32)) / (1.0 + PATCH * PATCH))
    offsets = ve_ref[...].astype(F32)
    for v in range(VPD):
        off_ref[v] = offsets[v : v + 1]
        bias_ref[v] = jnp.concatenate([bias[4 * v + row : 4 * v + row + 1] for row in rows], 1)
    w_copy(0).wait()
    px_copy(1).wait()
    for copy in small[2:]:
        copy.wait()
    if not edge:
        head = lax.broadcasted_iota(jnp.int32, (HEADS, D), 0)
        col = lax.broadcasted_iota(jnp.int32, (HEADS, D), 1)
        spread = jnp.where(col // HEAD == head, jnp.broadcast_to(query_ref[...], (HEADS, D)), 0.0)
        parts = lax.dot_general(jnp.concatenate(three_parts(spread), 0), key_ref[...], NT, preferred_element_type=F32)
        kq = (parts[0:8] + parts[8:16] + parts[16:24]) / math.sqrt(HEAD)
        ext[32 : D + 32, :] = value_ref[...].T
        ext[0:32, :] = jnp.concatenate((*three_parts(kq), jnp.zeros((8, D), BF)), 0)
        ext_copy = pltpu.make_async_copy(ext, ext_out.at[0 : D + 32], sem.at[0])
        ext_copy.start()
    embed_tokens(0, a_even, tok_even)
    relayout(1, a_odd, stage_odd)

    def pair(step, _):
        odd = 2 * step + 1

        @pl.when(step < VPD // 2 - 2)
        def _():
            for v in (odd + 2, odd + 3):
                w_copy(v).start()
                px_copy(v + 1).start()

        @pl.when(step == VPD // 2 - 2)
        def _():
            w_copy(VPD - 1).start()

        for v in (odd, odd + 1):
            w_copy(v).wait()
            px_copy(v + 1).wait()
        embed_tokens(odd, a_odd, tok_odd)
        attend(odd - 1, tok_even)
        relayout(odd + 1, a_even, stage_even)
        embed_tokens(odd + 1, a_even, tok_even)
        attend(odd, tok_odd)
        relayout(odd + 2, a_odd, stage_odd)
        return 0

    lax.fori_loop(0, VPD // 2 - 1, pair, 0)
    w_copy(VPD - 1).wait()
    embed_tokens(VPD - 1, a_odd, tok_odd)
    attend(VPD - 2, tok_even)
    attend(VPD - 1, tok_odd)
    if not edge:
        ext_copy.wait()

    lane = lax.broadcasted_iota(jnp.int32, (24, LANES), 1)
    total = tot_ref[...]
    parts = jnp.concatenate(three_parts(top_ref[...] + jnp.log(total)), 0)
    sums = []
    for n in range(2):
        half = slice(n * PC, (n + 1) * PC)
        weighted = jnp.concatenate(
            [acc_ref[h * HEAD : (h + 1) * HEAD, half] / total[h : h + 1, half] for h in range(HEADS)], 0
        ).astype(BF)
        natural = lax.dot_general(perm, weighted, NT, preferred_element_type=F32).astype(BF)
        for d in range(DEVS):
            msg_ref[d, n * OWN : (n + 1) * OWN, :] = natural[d * OWN : (d + 1) * OWN]
        sums.append(lax.dot_general(parts[:, half], perm, NT, preferred_element_type=F32))
    base = 2 * OWN if edge else 0
    for d in range(DEVS):
        spot = d * OWN // LANES * LANES
        picked = jnp.zeros((24, LANES), F32)
        for n in range(2):
            moved = pltpu.roll(sums[n][:, spot : spot + LANES], (base + n * OWN - d * OWN) % LANES, 1)
            picked = jnp.where(lane // OWN == base // OWN + n, moved, picked)
        wide = jnp.concatenate([picked[0:8], picked[8:16], picked[16:24], jnp.zeros((8, LANES), F32)], 1)
        msg_ref[d, 2 * OWN : MESSAGE, :] = wide.astype(BF)


def embed(edge, extras, pixels, weight, counts, var_embed):
    groups = 8 if edge else 6
    hbm = pl.BlockSpec(memory_space=pltpu.HBM)
    vmem = pl.BlockSpec(memory_space=pltpu.VMEM)
    out_shape = [jax.ShapeDtypeStruct((DEVS, MESSAGE, D), BF)]
    scratch = [
        pltpu.VMEM((VPD, 64, COLS), BF),
        pltpu.VMEM((VPD, 32, 32, D), BF),
        pltpu.VMEM((D + 32, D), BF),
        pltpu.VMEM((VPD, 4, PC), jnp.int32),
        pltpu.VMEM((VPD, D), BF),
        pltpu.VMEM((groups, PC + TILES, LANES), BF),
        pltpu.VMEM((groups, PC + TILES, LANES), BF),
        pltpu.VMEM((groups, TILES * 8, LANES), F32),
        pltpu.VMEM((groups, TILES * 8, LANES), F32),
        pltpu.VMEM((groups, TILES + 16, LANES), F32),
        pltpu.VMEM((D, D), BF),
        pltpu.VMEM((D, D), BF),
        pltpu.VMEM((VPD, 1, 2 * PC), F32),
        pltpu.VMEM((VPD, 1, D), F32),
        pltpu.VMEM((HEADS, 2 * PC), F32),
        pltpu.VMEM((HEADS, 2 * PC), F32),
        pltpu.VMEM((D, 2 * PC), F32),
        pltpu.SemaphoreType.DMA((VPD,)),
        pltpu.SemaphoreType.DMA((VPD,)),
        pltpu.SemaphoreType.DMA((5,)),
    ]
    if not edge:
        out_shape.append(jax.ShapeDtypeStruct((SPARE, D), BF))
        scratch += [pltpu.VMEM((1, D), F32), pltpu.VMEM((D, D), BF), pltpu.VMEM((D, D), BF)]
    return pl.pallas_call(
        functools.partial(embed_kernel, edge),
        in_specs=[vmem if edge else hbm] * 2 + [hbm] * 5,
        out_specs=[vmem, hbm][: len(out_shape)],
        out_shape=out_shape,
        scratch_shapes=scratch,
        compiler_params=pltpu.CompilerParams(vmem_limit_bytes=(52 if edge else 56) * 2**20),
        cost_estimate=pl.CostEstimate(flops=8 * 2 * 512 * (1024 + 512) * 512, bytes_accessed=13 * 2**20, transcendentals=0),
        name="embed_edge" if edge else "embed_inner",
    )(*extras, pixels, weight, counts, var_embed)


def finish_kernel(inner_ref, outer_ref, wo_ref, out_ref):
    lane = lax.broadcasted_iota(jnp.int32, (HEADS, LANES), 1)
    sums = []
    for s in range(DEVS):
        a = inner_ref[s, 2 * OWN : MESSAGE, :].astype(F32)
        b = outer_ref[s, 2 * OWN : MESSAGE, :].astype(F32)
        a = a[:, 0:LANES] + a[:, LANES : 2 * LANES] + a[:, 2 * LANES : 3 * LANES]
        b = b[:, 0:LANES] + b[:, LANES : 2 * LANES] + b[:, 2 * LANES : 3 * LANES]
        sums.append(jnp.where(lane < 2 * OWN, a, b))
    top = functools.reduce(jnp.maximum, sums)
    parts = [jnp.exp(x - top) for x in sums]
    scale = 1.0 / functools.reduce(jnp.add, parts)
    shares = []
    for part in parts:
        share = part * scale
        high = share.astype(BF).astype(F32)
        shares += [high, share - high]
    shares = jnp.concatenate(shares, 0).T.astype(BF)
    row = lax.broadcasted_iota(jnp.int32, (LANES, D), 0)
    col = lax.broadcasted_iota(jnp.int32, (LANES, D), 1)
    spread = jnp.where((row < 16) & (col // HEAD == row % HEADS), 1.0, 0.0).astype(BF)
    turned = [pltpu.roll(shares, (-16 * s) % LANES, 1) if s else shares for s in range(DEVS)]
    wide = jnp.dot(jnp.concatenate(turned, 0), spread, preferred_element_type=F32)
    mixture = jnp.zeros((LANES, D), F32)
    for s in range(DEVS):
        values = jnp.concatenate([inner_ref[s, 0 : 2 * OWN, :], outer_ref[s, 0 : 2 * OWN, :]], 0)
        mixture = mixture + wide[s * LANES : (s + 1) * LANES] * values.astype(F32)
    result = jnp.dot(mixture.astype(BF), wo_ref[...], preferred_element_type=F32).astype(BF)
    for n, row in enumerate((1, 2, 0, 3)):
        out_ref[row] = result[n * OWN : (n + 1) * OWN]


def finish(inner, outer, out_weight):
    return pl.pallas_call(
        finish_kernel,
        out_shape=jax.ShapeDtypeStruct((4, OWN, D), BF),
        compiler_params=pltpu.CompilerParams(vmem_limit_bytes=24 * 2**20),
        cost_estimate=pl.CostEstimate(flops=2 * 128 * 512 * 512, bytes_accessed=2**21, transcendentals=0),
        name="finish",
    )(inner, outer, out_weight)


def exchange(msg):
    return lax.all_to_all(msg, "var", 0, 0)


def shards(pixels, counts, embed_weight, var_embed, query, key_weight, value_weight, out_weight):
    count = lax.axis_size("space")
    odd = lax.rem(lax.axis_index("space"), 2)
    far_pairs = [(i, i + 1) for i in range(1, count - 1, 2)]
    near_pairs = [(i, i + 1) for i in range(0, count - 1, 2)]
    both_ways = lambda pairs: pairs + [(b, a) for a, b in pairs]
    reach = PATCH // 2
    last = pixels.shape[1] - reach
    far = lax.ppermute(lax.dynamic_slice_in_dim(pixels, odd * last, reach, 1), "space", both_ways(far_pairs))
    near = lax.ppermute(lax.dynamic_slice_in_dim(pixels, (1 - odd) * last, reach, 1), "space", both_ways(near_pairs))
    rest = (pixels, embed_weight, counts, var_embed)
    inner, ext = embed(False, (query.reshape(1, D), key_weight, value_weight), *rest)
    inner = exchange(inner)
    (outer,) = embed(True, (far, near, ext), *rest)
    outer = exchange(outer)
    return finish(inner, outer, out_weight)


def solution(mesh):
    return jax.shard_map(
        shards,
        mesh=mesh,
        in_specs=(
            P("var", "space", None),
            P("var", "space", None),
            P("var", None, None, None),
            P("var", None),
            P(),
            P(),
            P(),
            P(),
        ),
        out_specs=P("space", "var", None),
        check_vma=False,
    )
```

```python
import functools
import math

import jax
import jax.numpy as jnp
from jax import lax
from jax.experimental import pallas as pl
from jax.experimental.pallas import tpu as pltpu
from jax.sharding import PartitionSpec as P

HEADS = 8
HEAD = 64
PATCH = 16
D = 512
COLS = 4096
PC = 256
LANES = 128
TILES = COLS // LANES
VPD = 8
DEVS = 8
OWN = PC // DEVS
MESSAGE = 2 * OWN + 8
BF = jnp.bfloat16
F32 = jnp.float32
NT = (((1,), (1,)), ((), ()))
SPARE = 8192


def three_parts(x):
    high = x.astype(BF)
    rest = x - high.astype(F32)
    middle = rest.astype(BF)
    return high, middle, (rest - middle.astype(F32)).astype(BF)


def relayout_group(rows, stage, edge_stage, out):
    for t in range(TILES):
        stage[t * 8 : t * 8 + 8, :] = rows[:, t * LANES : (t + 1) * LANES]
    skewed = [
        pltpu.roll(stage[pl.ds(r, TILES, stride=8), :].astype(BF), (16 * r + 8) % LANES, 1) for r in range(8)
    ]
    lane = lax.broadcasted_iota(jnp.int32, (TILES, LANES), 1)
    level = [skewed[(-k) % 8] for k in range(8)]
    for bit in (1, 2, 4):
        chosen = ((lane // 16) & bit) != 0
        level = [jnp.where(chosen, level[(k - bit) % 8], level[k]) for k in range(8)]
    for k in range(1, 8):
        out[k * TILES : (k + 1) * TILES, :] = pltpu.roll(level[k], (-16 * k) % LANES, 1)
    edge_stage[8 : 8 + TILES, :] = level[0].astype(F32)
    left = (lane % 16) < 8
    out[0:TILES, :] = jnp.where(left, edge_stage[7 : 7 + TILES, :].astype(BF), level[0])
    out[8 * TILES : 9 * TILES, :] = jnp.where(left, level[0], edge_stage[9 : 9 + TILES, :].astype(BF))


def permutation():
    row = lax.broadcasted_iota(jnp.int32, (PC, PC), 0)
    col = lax.broadcasted_iota(jnp.int32, (PC, PC), 1)
    same = ((row // 8) == (col % TILES)) & ((row % 8) == (col // TILES))
    return jnp.where(same, 1.0, 0.0).astype(BF)


def embed_kernel(edge, *refs):
    if edge:
        far_ref, near_ref, ext_hbm, *refs = refs
        odd_tile = lax.rem(lax.axis_index("space"), 2) == 1
    else:
        query_hbm, key_hbm, value_hbm, *refs = refs
    px_hbm, w_hbm, cnt_hbm, ve_hbm, msg_ref, *refs = refs
    if not edge:
        msg_hbm = msg_ref
        ext_out, *refs = refs
    (px, w, ext, cnt_ref, ve_ref, a_even, a_odd, stage_even, stage_odd, edges, tok_even, tok_odd, bias_ref, off_ref,
     top_ref, tot_ref, acc_ref, px_sem, w_sem, sem, *more) = refs
    rows = (0, 3) if edge else (1, 2)
    starts = (0, 4) if edge else (0, 2)

    def px_copy(v):
        return pltpu.make_async_copy(px_hbm.at[v], px.at[v], px_sem.at[v])

    def w_copy(v):
        return pltpu.make_async_copy(w_hbm.at[v], w.at[v], w_sem.at[v])

    small = [(cnt_hbm, cnt_ref), (ve_hbm, ve_ref)]
    if edge:
        small.append((ext_hbm.at[0 : D + 32], ext))
    else:
        query_ref, key_ref, value_ref, msg_ref, msg_sem = more
        small += [(query_hbm, query_ref), (key_hbm, key_ref), (value_hbm, value_ref)]
    small = [pltpu.make_async_copy(src, dst, sem.at[n]) for n, (src, dst) in enumerate(small)]
    px_copy(0).start()
    for copy in small:
        copy.start()
    w_copy(0).start()
    px_copy(1).start()

    def relayout(v, a_ref, stage):
        body = px[v].astype(F32)
        if edge:
            far, near = far_ref[v].astype(F32), near_ref[v].astype(F32)
            groups = [jnp.where(odd_tile, near, far), body[0:8], body[8:16], body[16:24],
                      body[40:48], body[48:56], body[56:64], jnp.where(odd_tile, far, near)]
        else:
            groups = [body[8 * n : 8 * n + 8] for n in range(1, 7)]
        for n, group in enumerate(groups):
            relayout_group(group, stage.at[n], edges.at[n], a_ref.at[n])

    def embed_tokens(v, a_ref, tok):
        a = jnp.concatenate(
            [
                jnp.concatenate([a_ref[start + g, b * TILES : b * TILES + PC, :] for g in range(4) for b in range(2)], 1)
                for start in starts
            ],
            0,
        )
        weight = jnp.concatenate(
            [w[v, 8 * g : 8 * g + 8, 16 * b : 16 * b + 16, :].reshape(LANES, D) for g in range(4) for b in range(2)], 0
        )
        tok[...] = (jnp.dot(a, weight, preferred_element_type=F32) + off_ref[v]).astype(BF)

    def attend(v, tok):
        both = lax.dot_general(ext[...], tok[...], NT, preferred_element_type=F32)
        scores = both[0:8] + both[8:16] + both[16:24] + bias_ref[v]
        old = top_ref[...]
        top = jnp.maximum(old, scores)
        decay = jnp.exp(old - top)
        fresh = jnp.exp(scores - top)
        top_ref[...] = top
        tot_ref[...] = tot_ref[...] * decay + fresh
        for h in range(HEADS):
            at = slice(h * HEAD, (h + 1) * HEAD)
            acc_ref[at, :] = acc_ref[at, :] * decay[h : h + 1] + both[32 + h * HEAD : 32 + (h + 1) * HEAD] * fresh[h : h + 1]

    edges[...] = jnp.zeros_like(edges)
    perm = permutation()
    top_ref[...] = jnp.full_like(top_ref, -1e30)
    tot_ref[...] = jnp.zeros_like(tot_ref)
    acc_ref[...] = jnp.zeros_like(acc_ref)
    px_copy(0).wait()
    w_copy(1).start()
    px_copy(2).start()
    relayout(0, a_even, stage_even)
    w_copy(2).start()
    px_copy(3).start()
    small[0].wait()
    small[1].wait()
    valid = jnp.concatenate([cnt_ref[v].astype(F32) for v in range(VPD)], 0).astype(BF)
    bias = jnp.log((1.0 + jnp.dot(valid, perm, preferred_element_type=F32)) / (1.0 + PATCH * PATCH))
    offsets = ve_ref[...].astype(F32)
    for v in range(VPD):
        off_ref[v] = offsets[v : v + 1]
        bias_ref[v] = jnp.concatenate([bias[4 * v + row : 4 * v + row + 1] for row in rows], 1)
    w_copy(0).wait()
    px_copy(1).wait()
    for copy in small[2:]:
        copy.wait()
    if not edge:
        head = lax.broadcasted_iota(jnp.int32, (HEADS, D), 0)
        col = lax.broadcasted_iota(jnp.int32, (HEADS, D), 1)
        spread = jnp.where(col // HEAD == head, jnp.broadcast_to(query_ref[...], (HEADS, D)), 0.0)
        parts = lax.dot_general(jnp.concatenate(three_parts(spread), 0), key_ref[...], NT, preferred_element_type=F32)
        kq = (parts[0:8] + parts[8:16] + parts[16:24]) / math.sqrt(HEAD)
        ext[32 : D + 32, :] = value_ref[...].T
        ext[0:32, :] = jnp.concatenate((*three_parts(kq), jnp.zeros((8, D), BF)), 0)
        ext_copy = pltpu.make_async_copy(ext, ext_out.at[0 : D + 32], sem.at[0])
        ext_copy.start()
    embed_tokens(0, a_even, tok_even)
    relayout(1, a_odd, stage_odd)

    def pair(step, _):
        odd = 2 * step + 1

        @pl.when(step < VPD // 2 - 2)
        def _():
            for v in (odd + 2, odd + 3):
                w_copy(v).start()
                px_copy(v + 1).start()

        @pl.when(step == VPD // 2 - 2)
        def _():
            w_copy(VPD - 1).start()

        for v in (odd, odd + 1):
            w_copy(v).wait()
            px_copy(v + 1).wait()
        embed_tokens(odd, a_odd, tok_odd)
        attend(odd - 1, tok_even)
        relayout(odd + 1, a_even, stage_even)
        embed_tokens(odd + 1, a_even, tok_even)
        attend(odd, tok_odd)
        relayout(odd + 2, a_odd, stage_odd)
        return 0

    lax.fori_loop(0, VPD // 2 - 1, pair, 0)
    w_copy(VPD - 1).wait()
    embed_tokens(VPD - 1, a_odd, tok_odd)
    attend(VPD - 2, tok_even)
    attend(VPD - 1, tok_odd)
    if not edge:
        ext_copy.wait()

    lane = lax.broadcasted_iota(jnp.int32, (24, LANES), 1)
    total = tot_ref[...]
    parts = jnp.concatenate(three_parts(top_ref[...] + jnp.log(total)), 0)
    sums, row_copies = [], []
    for n in range(2):
        half = slice(n * PC, (n + 1) * PC)
        weighted = jnp.concatenate(
            [acc_ref[h * HEAD : (h + 1) * HEAD, half] / total[h : h + 1, half] for h in range(HEADS)], 0
        ).astype(BF)
        natural = lax.dot_general(perm, weighted, NT, preferred_element_type=F32).astype(BF)
        for d in range(DEVS):
            msg_ref[d, n * OWN : (n + 1) * OWN, :] = natural[d * OWN : (d + 1) * OWN]
        if not edge:
            at = pl.ds(n * OWN, OWN)
            row_copies.append(pltpu.make_async_copy(msg_ref.at[:, at], msg_hbm.at[:, at], msg_sem.at[n]))
            row_copies[-1].start()
        sums.append(lax.dot_general(parts[:, half], perm, NT, preferred_element_type=F32))
    base = 2 * OWN if edge else 0
    for d in range(DEVS):
        spot = d * OWN // LANES * LANES
        picked = jnp.zeros((24, LANES), F32)
        for n in range(2):
            moved = pltpu.roll(sums[n][:, spot : spot + LANES], (base + n * OWN - d * OWN) % LANES, 1)
            picked = jnp.where(lane // OWN == base // OWN + n, moved, picked)
        wide = jnp.concatenate([picked[0:8], picked[8:16], picked[16:24], jnp.zeros((8, LANES), F32)], 1)
        msg_ref[d, 2 * OWN : MESSAGE, :] = wide.astype(BF)
    if not edge:
        at = pl.ds(2 * OWN, MESSAGE - 2 * OWN)
        row_copies.append(pltpu.make_async_copy(msg_ref.at[:, at], msg_hbm.at[:, at], msg_sem.at[2]))
        row_copies[-1].start()
        for copy in row_copies:
            copy.wait()


def embed(edge, extras, pixels, weight, counts, var_embed):
    groups = 8 if edge else 6
    hbm = pl.BlockSpec(memory_space=pltpu.HBM)
    vmem = pl.BlockSpec(memory_space=pltpu.VMEM)
    out_shape = [jax.ShapeDtypeStruct((DEVS, MESSAGE, D), BF)]
    scratch = [
        pltpu.VMEM((VPD, 64, COLS), BF),
        pltpu.VMEM((VPD, 32, 32, D), BF),
        pltpu.VMEM((D + 32, D), BF),
        pltpu.VMEM((VPD, 4, PC), jnp.int32),
        pltpu.VMEM((VPD, D), BF),
        pltpu.VMEM((groups, PC + TILES, LANES), BF),
        pltpu.VMEM((groups, PC + TILES, LANES), BF),
        pltpu.VMEM((groups, TILES * 8, LANES), F32),
        pltpu.VMEM((groups, TILES * 8, LANES), F32),
        pltpu.VMEM((groups, TILES + 16, LANES), F32),
        pltpu.VMEM((D, D), BF),
        pltpu.VMEM((D, D), BF),
        pltpu.VMEM((VPD, 1, 2 * PC), F32),
        pltpu.VMEM((VPD, 1, D), F32),
        pltpu.VMEM((HEADS, 2 * PC), F32),
        pltpu.VMEM((HEADS, 2 * PC), F32),
        pltpu.VMEM((D, 2 * PC), F32),
        pltpu.SemaphoreType.DMA((VPD,)),
        pltpu.SemaphoreType.DMA((VPD,)),
        pltpu.SemaphoreType.DMA((5,)),
    ]
    if not edge:
        out_shape.append(jax.ShapeDtypeStruct((SPARE, D), BF))
        scratch += [
            pltpu.VMEM((1, D), F32),
            pltpu.VMEM((D, D), BF),
            pltpu.VMEM((D, D), BF),
            pltpu.VMEM((DEVS, MESSAGE, D), BF),
            pltpu.SemaphoreType.DMA((3,)),
        ]
    return pl.pallas_call(
        functools.partial(embed_kernel, edge),
        in_specs=[vmem if edge else hbm] * 2 + [hbm] * 5,
        out_specs=[vmem] if edge else [hbm, hbm],
        out_shape=out_shape,
        scratch_shapes=scratch,
        compiler_params=pltpu.CompilerParams(vmem_limit_bytes=(52 if edge else 56) * 2**20),
        cost_estimate=pl.CostEstimate(flops=8 * 2 * 512 * (1024 + 512) * 512, bytes_accessed=13 * 2**20, transcendentals=0),
        name="embed_edge" if edge else "embed_inner",
    )(*extras, pixels, weight, counts, var_embed)


def finish_kernel(inner_ref, outer_ref, wo_ref, out_ref):
    lane = lax.broadcasted_iota(jnp.int32, (HEADS, LANES), 1)
    sums = []
    for s in range(DEVS):
        a = inner_ref[s, 2 * OWN : MESSAGE, :].astype(F32)
        b = outer_ref[s, 2 * OWN : MESSAGE, :].astype(F32)
        a = a[:, 0:LANES] + a[:, LANES : 2 * LANES] + a[:, 2 * LANES : 3 * LANES]
        b = b[:, 0:LANES] + b[:, LANES : 2 * LANES] + b[:, 2 * LANES : 3 * LANES]
        sums.append(jnp.where(lane < 2 * OWN, a, b))
    top = functools.reduce(jnp.maximum, sums)
    parts = [jnp.exp(x - top) for x in sums]
    scale = 1.0 / functools.reduce(jnp.add, parts)
    shares = []
    for part in parts:
        share = part * scale
        high = share.astype(BF).astype(F32)
        shares += [high, share - high]
    shares = jnp.concatenate(shares, 0).T.astype(BF)
    row = lax.broadcasted_iota(jnp.int32, (LANES, D), 0)
    col = lax.broadcasted_iota(jnp.int32, (LANES, D), 1)
    spread = jnp.where((row < 16) & (col // HEAD == row % HEADS), 1.0, 0.0).astype(BF)
    turned = [pltpu.roll(shares, (-16 * s) % LANES, 1) if s else shares for s in range(DEVS)]
    wide = jnp.dot(jnp.concatenate(turned, 0), spread, preferred_element_type=F32)
    mixture = jnp.zeros((LANES, D), F32)
    for s in range(DEVS):
        values = jnp.concatenate([inner_ref[s, 0 : 2 * OWN, :], outer_ref[s, 0 : 2 * OWN, :]], 0)
        mixture = mixture + wide[s * LANES : (s + 1) * LANES] * values.astype(F32)
    result = jnp.dot(mixture.astype(BF), wo_ref[...], preferred_element_type=F32).astype(BF)
    for n, row in enumerate((1, 2, 0, 3)):
        out_ref[row] = result[n * OWN : (n + 1) * OWN]


def finish(inner, outer, out_weight):
    return pl.pallas_call(
        finish_kernel,
        out_shape=jax.ShapeDtypeStruct((4, OWN, D), BF),
        compiler_params=pltpu.CompilerParams(vmem_limit_bytes=24 * 2**20),
        cost_estimate=pl.CostEstimate(flops=2 * 128 * 512 * 512, bytes_accessed=2**21, transcendentals=0),
        name="finish",
    )(inner, outer, out_weight)


def exchange(msg):
    return lax.all_to_all(msg, "var", 0, 0)


def shards(pixels, counts, embed_weight, var_embed, query, key_weight, value_weight, out_weight):
    count = lax.axis_size("space")
    odd = lax.rem(lax.axis_index("space"), 2)
    far_pairs = [(i, i + 1) for i in range(1, count - 1, 2)]
    near_pairs = [(i, i + 1) for i in range(0, count - 1, 2)]
    both_ways = lambda pairs: pairs + [(b, a) for a, b in pairs]
    reach = PATCH // 2
    last = pixels.shape[1] - reach
    far = lax.ppermute(lax.dynamic_slice_in_dim(pixels, odd * last, reach, 1), "space", both_ways(far_pairs))
    near = lax.ppermute(lax.dynamic_slice_in_dim(pixels, (1 - odd) * last, reach, 1), "space", both_ways(near_pairs))
    rest = (pixels, embed_weight, counts, var_embed)
    inner, ext = embed(False, (query.reshape(1, D), key_weight, value_weight), *rest)
    inner = exchange(inner)
    (outer,) = embed(True, (far, near, ext), *rest)
    outer = exchange(outer)
    return finish(inner, outer, out_weight)


def solution(mesh):
    return jax.shard_map(
        shards,
        mesh=mesh,
        in_specs=(
            P("var", "space", None),
            P("var", "space", None),
            P("var", None, None, None),
            P("var", None),
            P(),
            P(),
            P(),
            P(),
        ),
        out_specs=P("space", "var", None),
        check_vma=False,
    )
```
